32 devices in a mesh: row: 4 (over y, core), col: 8 (over z, x).
Axes of the slice: x: 2, y: 2, z: 4, core: 2. Of those that a mesh axis runs over, the one named last changes fastest.
Arguments:
- student_image: bfloat16 [2048, 512], P(('row', 'col')), may hold values from -0.16 to 0.16
- student_text: bfloat16 [2048, 512], P(('row', 'col')), may hold values from -0.16 to 0.16
- teacher_image: bfloat16 [2048, 1280], P(('row', 'col')), may hold values from -32 to 32
- teacher_text: bfloat16 [2048, 1280], P(('row', 'col')), may hold values from -32 to 32
- teacher_scale: float32 [], replicated, may hold values from 20 to 250
- student_scale: float32 [], replicated, may hold values from 10 to 250
Outputs:
- image_grad: float32 [2048, 512], P(('row', 'col'))
- text_grad: float32 [2048, 512], P(('row', 'col'))
The draws below stay inside these ranges and needn't reach their ends.
All inputs are finite; a program needn't handle non-finite values.
Results may differ from the reference program's by a relative error of at most 0.012.
The reference program's roundings to bfloat16 on the way (of `weight`) count: a program that leaves them out, or rounds other values in their place, can miss the bound.
Values may be sent and summed in bfloat16 or wider, within the bound.
No kernel may reach another device: no remote copies, remote signals or barrier semaphores. Data moves between devices by JAX's collectives and lax.ppermute only.
A program may use at most 64 MiB of HBM per device.

```python
import jax
import jax.numpy as jnp
from jax import lax

DS = 512
DT = 1280
BATCH = 2048


def embedding_rows(key, rows, width, factor):
    own_draw = jnp.clip(jax.random.normal(key, (rows, width), jnp.float32), -8.0, 8.0)
    return (own_draw * factor).astype(jnp.bfloat16)


def draw_teacher_image(key, part):
    key = jax.random.fold_in(key, 1)
    return embedding_rows(key, BATCH, DT, 1.0)


def draw_teacher_text(key, part):
    key = jax.random.fold_in(key, 2)
    return embedding_rows(key, BATCH, DT, 1.0)


def draw_student_image(key, part):
    key = jax.random.fold_in(key, 3)
    return embedding_rows(key, BATCH, DS, 0.005)


def draw_student_text(key, part):
    key = jax.random.fold_in(key, 4)
    return embedding_rows(key, BATCH, DS, 0.005)


def draw_teacher_scale(key, part):
    key = jax.random.fold_in(key, 5)
    return jax.random.uniform(key, (), jnp.float32, 20.0, 100.0)


def draw_student_scale(key, part):
    key = jax.random.fold_in(key, 6)
    return jax.random.uniform(key, (), jnp.float32, 10.0, 60.0)


def setup_inputs(seed: int = 0) -> dict:
    arg_keys = jax.random.split(jax.random.key(seed), 7)
    return {
        "student_image": draw_student_image(jax.random.fold_in(arg_keys[6], 71), 0),
        "student_text": draw_student_text(jax.random.fold_in(arg_keys[6], 71), 0),
        "teacher_image": draw_teacher_image(jax.random.fold_in(arg_keys[6], 71), 0),
        "teacher_text": draw_teacher_text(jax.random.fold_in(arg_keys[6], 71), 0),
        "teacher_scale": draw_teacher_scale(jax.random.fold_in(arg_keys[6], 71), 0),
        "student_scale": draw_student_scale(jax.random.fold_in(arg_keys[6], 71), 0),
    }


EPSILON = 1e-12

def unit_rows(raw):
    values = raw.astype(jnp.float32)
    inverse = lax.rsqrt(lax.optimization_barrier(jnp.sum(values * values, axis=-1, keepdims=True)) + EPSILON)
    return (values * inverse, inverse)

def scaled_logits(left, right, scale):
    product = lax.dot_general(left, right, (((1,), (1,)), ((), ())), precision=lax.Precision.HIGHEST, preferred_element_type=jnp.float32)
    return scale * product

def block_stats(logits, axis):
    peak = lax.optimization_barrier(jnp.max(logits, axis=axis))
    total = lax.optimization_barrier(jnp.sum(jnp.exp(logits - jnp.expand_dims(peak, axis)), axis=axis))
    return (peak, total)

def join_pair(peak_a, total_a, peak_b, total_b):
    top = jnp.maximum(peak_a, peak_b)
    return (top, total_a * jnp.exp(peak_a - top) + total_b * jnp.exp(peak_b - top))

def join_stats(first, second):
    teach_peak, teach_total = join_pair(first[0], first[1], second[0], second[1])
    learn_peak, learn_total = join_pair(first[2], first[3], second[2], second[3])
    return (teach_peak, teach_total, learn_peak, learn_total)

def back_norm(grad, unit, inverse):
    return inverse * (grad - unit * lax.optimization_barrier(jnp.sum(unit * grad, axis=-1, keepdims=True)))

def reference(student_image, student_text, teacher_image, teacher_text, teacher_scale, student_scale):
    image_unit, image_inverse = unit_rows(student_image)
    text_unit, text_inverse = unit_rows(student_text)
    pupil_image = image_unit.astype(jnp.bfloat16)
    pupil_text = text_unit.astype(jnp.bfloat16)
    master_image = unit_rows(teacher_image)[0].astype(jnp.bfloat16)
    master_text = unit_rows(teacher_text)[0].astype(jnp.bfloat16)
    rows_block = min(512, BATCH)
    blocks = BATCH // rows_block
    master_blocks = master_image.astype(jnp.float32).reshape(blocks, rows_block, DT)
    pupil_blocks = pupil_image.astype(jnp.float32).reshape(blocks, rows_block, DS)
    master_cols = master_text.astype(jnp.float32)
    pupil_cols = pupil_text.astype(jnp.float32)

    def first_pass(carried, pieces):
        master_piece, pupil_piece = pieces
        teach = scaled_logits(master_piece, master_cols, teacher_scale)
        learn = scaled_logits(pupil_piece, pupil_cols, student_scale)
        teach_peak, teach_total = block_stats(teach, 0)
        learn_peak, learn_total = block_stats(learn, 0)
        updated = join_stats(carried, (teach_peak, teach_total, learn_peak, learn_total))
        return (updated, block_stats(teach, 1) + block_stats(learn, 1))
    lowest = jnp.full((BATCH,), -jnp.inf, jnp.float32)
    nothing = jnp.zeros((BATCH,), jnp.float32)
    column_stats, row_stats = lax.scan(first_pass, (lowest, nothing, lowest, nothing), (master_blocks, pupil_blocks))

    def second_pass(carried, pieces):
        master_piece, pupil_piece, teach_peak, teach_total, learn_peak, learn_total = pieces
        teach = scaled_logits(master_piece, master_cols, teacher_scale)
        learn = scaled_logits(pupil_piece, pupil_cols, student_scale)
        rows_part = jnp.exp(learn - learn_peak[:, None]) / learn_total[:, None] - jnp.exp(teach - teach_peak[:, None]) / teach_total[:, None]
        cols_part = jnp.exp(learn - column_stats[2][None, :]) / column_stats[3][None, :] - jnp.exp(teach - column_stats[0][None, :]) / column_stats[1][None, :]
        weight = (0.5 * (rows_part + cols_part)).astype(jnp.bfloat16).astype(jnp.float32)
        image_part = student_scale * jnp.dot(weight, pupil_cols, precision=lax.Precision.HIGHEST, preferred_element_type=jnp.float32)
        text_part = student_scale * lax.dot_general(weight, pupil_piece, (((0,), (0,)), ((), ())), precision=lax.Precision.HIGHEST, preferred_element_type=jnp.float32)
        return (carried + text_part, image_part)
    text_unit_grad, image_parts = lax.scan(second_pass, jnp.zeros((BATCH, DS), jnp.float32), (master_blocks, pupil_blocks) + tuple(row_stats))
    image_unit_grad = image_parts.reshape(BATCH, DS)
    return (back_norm(image_unit_grad, image_unit, image_inverse), back_norm(text_unit_grad, text_unit, text_inverse))
```

```python
import functools

import jax
import jax.numpy as jnp
from jax import lax
from jax.experimental import pallas as pl
from jax.experimental.pallas import tpu as pltpu
from jax.sharding import Mesh, PartitionSpec as P

EPSILON = 1e-12
SQUARE = ("y", "x")
PLANE = ("core", "y", "x")
LINE = "z"
EVERY = ("y", "core", "z", "x")
F32 = jnp.float32
BF16 = jnp.bfloat16
MANY = 1 << 35


def physical_mesh(mesh):
    rows, cols = mesh.shape["row"], mesh.shape["col"]
    side = rows // 2
    wide = side if cols % side == 0 else 1
    return Mesh(mesh.devices.reshape(side, 2, cols // wide, wide), EVERY)


def unit_rows(raw):
    values = raw.astype(F32)
    inverse = lax.rsqrt(jnp.sum(values * values, axis=-1, keepdims=True) + EPSILON)
    return (values * inverse, inverse)


def put_units(block, pupil_ref, master_ref, at):
    own, width = block.shape[0], pupil_ref.shape[1]
    pupil_ref[pl.ds(at, own), :] = unit_rows(block[:, :width])[0].astype(BF16)
    master_ref[pl.ds(at, own), :] = unit_rows(block[:, width:])[0].astype(BF16)


def image_unit_kernel(core_ref, square_ref, *refs):
    pupil_ref, master_ref = refs[-2:]
    blocks = refs[:-2]
    own = blocks[0].shape[0]
    squares = len(blocks) // 2
    core = core_ref[0]
    for s in range(squares):
        at = jnp.bitwise_xor(square_ref[0], s)
        for ref, half in ((blocks[s], core), (blocks[squares + s], 1 - core)):
            row = pl.multiple_of((half * squares + at) * own, own)
            put_units(ref[...], pupil_ref, master_ref, row)


def text_unit_kernel(z_ref, *refs):
    pupil_ref, master_ref = refs[-2:]
    own = refs[0].shape[0]
    for s, ref in enumerate(refs[:-2]):
        row = pl.multiple_of(jnp.bitwise_xor(z_ref[0], s) * own, own)
        put_units(ref[...], pupil_ref, master_ref, row)


def product(left, right):
    return lax.dot_general(left, right, (((1,), (1,)), ((), ())), preferred_element_type=F32)


def block_lse(logits):
    peak = jnp.max(logits, axis=0, keepdims=True)
    return peak + jnp.log(jnp.sum(jnp.exp(logits - peak), axis=0, keepdims=True))


def join_lse(parts):
    top = functools.reduce(jnp.maximum, parts)
    return top + jnp.log(sum(jnp.exp(p - top) for p in parts))


def logits_kernel(
    teacher_scale_ref, student_scale_ref, pupil_text_ref, master_text_ref, pupil_image_ref,
    master_image_ref, teach_ref, rows_ref, cols_ref,
):
    images = pupil_image_ref.shape[0]
    step = min(512, images)
    for k, (scale_ref, image_ref, text_ref) in enumerate(
        (
            (teacher_scale_ref, master_image_ref, master_text_ref),
            (student_scale_ref, pupil_image_ref, pupil_text_ref),
        )
    ):
        scale = scale_ref[0]
        text = text_ref[...]
        columns = []
        for at in range(0, images, step):
            image = image_ref[at : at + step, :]
            logits = scale * product(image, text)
            if k == 0:
                teach_ref[at : at + step, :] = logits
            columns.append(block_lse(logits))
            row = block_lse(scale * product(text, image))
            for i in range(rows_ref.shape[0]):
                rows_ref[i, k : k + 1, at : at + step] = row
        cols_ref[k : k + 1, :] = join_lse(columns)


def join_kernel(rows_ref, out_ref):
    joined = join_lse([rows_ref[i] for i in range(rows_ref.shape[0])])
    for k in range(0, 8, 2):
        out_ref[k : k + 2, :] = joined


def weight_kernel(depth, z_ref, scale_ref, teach_ref, image_ref, text_ref, rows_ref, *refs):
    col_refs = refs[:depth]
    image_out_ref, own_text_ref = refs[depth : depth + 2]
    text_out_refs = refs[depth + 2 : -1]
    text_part_ref = refs[-1]
    plane, own, _ = image_out_ref.shape
    z = z_ref[0]
    scale = scale_ref[0]
    images = plane * own
    step = min(512, images)
    col = join_lse([ref[...] for ref in col_refs])
    text = text_ref[...]
    for at in range(0, images, step):
        row = jnp.transpose(rows_ref[:, at : at + step])
        image = image_ref[at : at + step, :]
        teach = teach_ref[at : at + step, :]
        learn = scale * product(image, text)
        rows_part = jnp.exp(learn - row[:, 1:2]) - jnp.exp(teach - row[:, 0:1])
        cols_part = jnp.exp(learn - col[1:2, :]) - jnp.exp(teach - col[0:1, :])
        weight = (0.5 * (rows_part + cols_part)).astype(BF16)
        image_part = scale * jnp.dot(weight, text, preferred_element_type=F32)
        for i in range(step // own):
            image_out_ref[at // own + i] = image_part[i * own : (i + 1) * own].astype(BF16)
        text_part = scale * lax.dot_general(
            weight, image, (((0,), (0,)), ((), ())), preferred_element_type=F32
        )
        if at:
            text_part = text_part_ref[...] + text_part
        text_part_ref[...] = text_part
    own_text_ref[...] = text_part_ref[pl.ds(pl.multiple_of(z * own, own), own), :]
    for s in range(1, depth):
        at = pl.multiple_of(jnp.bitwise_xor(z, s) * own, own)
        text_out_refs[s - 1][...] = text_part_ref[pl.ds(at, own), :].astype(BF16)


def back_norm(grad, raw):
    unit, inverse = unit_rows(raw)
    return inverse * (grad - unit * jnp.sum(unit * grad, axis=-1, keepdims=True))


def sum_kernel(parts_ref, out_ref):
    grad = parts_ref[0].astype(F32)
    for i in range(1, parts_ref.shape[0]):
        grad = grad + parts_ref[i].astype(F32)
    out_ref[...] = grad


def back_kernel(image_ref, raw_image_ref, raw_text_ref, *refs):
    image_out_ref, text_out_ref = refs[-2:]
    grad = refs[0][...]
    for ref in refs[1:-2]:
        grad = grad + ref[...].astype(F32)
    text_out_ref[...] = back_norm(grad, raw_text_ref[...])
    image_out_ref[...] = back_norm(image_ref[...], raw_image_ref[...])


def shaped(shape, dtype):
    return jax.ShapeDtypeStruct(shape, dtype)


def call(kernel, outs, ins, specs, out_spec, scratch=(), grant=16, flops=1 << 20):
    return pl.pallas_call(
        kernel,
        out_shape=outs,
        in_specs=specs,
        out_specs=jax.tree.map(lambda _: out_spec, outs),
        scratch_shapes=list(scratch),
        compiler_params=pltpu.CompilerParams(vmem_limit_bytes=grant << 20),
        cost_estimate=pl.CostEstimate(flops=flops, bytes_accessed=1 << 20, transcendentals=0),
    )(*ins)


def make_body(squares, depth):
    plane = 2 * squares
    vmem = pl.BlockSpec(memory_space=pltpu.VMEM)
    smem = pl.BlockSpec(memory_space=pltpu.SMEM)

    def to_line(value, step):
        return lax.ppermute(value, LINE, [(z, z ^ step) for z in range(depth)])

    def to_square(value, step):
        return lax.ppermute(value, SQUARE, [(q, q ^ step) for q in range(squares)])

    def gather_line(value):
        blocks = {0: value}
        for s in sorted(range(1, depth), key=lambda s: bin(s).count("1")):
            near = s & -s
            blocks[s] = to_line(blocks[s ^ near], near)
        return [blocks[s] for s in range(depth)]

    def exchange(value, axes):
        return lax.all_to_all(value, axes, split_axis=0, concat_axis=0, tiled=True)

    def body(student_image, student_text, teacher_image, teacher_text, teacher_scale, student_scale):
        own, width = student_image.shape
        both = width + teacher_image.shape[1]
        images, texts = plane * own, depth * own
        core = lax.axis_index("core").astype(jnp.int32).reshape(1)
        square = lax.axis_index("y") * lax.axis_size("x") + lax.axis_index("x")
        square = square.astype(jnp.int32).reshape(1)
        z = lax.axis_index("z").astype(jnp.int32).reshape(1)
        teacher_scale = teacher_scale.reshape(1)
        student_scale = student_scale.reshape(1)
        grant = 16 if images * texts <= 512 * 256 else 56

        raw_text = jnp.concatenate([student_text, teacher_text], 1)
        raw_texts = gather_line(raw_text)
        raw_image = jnp.concatenate([student_image, teacher_image], 1)
        same = [raw_image] + [to_square(raw_image, s) for s in range(1, squares)]
        other = [lax.ppermute(block, "core", [(0, 1), (1, 0)]) for block in same]

        pupil_text, master_text = call(
            text_unit_kernel,
            (shaped((texts, width), BF16), shaped((texts, both - width), BF16)),
            (z, *raw_texts),
            [smem] + [vmem] * depth,
            vmem,
            grant=grant,
            flops=MANY,
        )
        pupil_image, master_image = call(
            image_unit_kernel,
            (shaped((images, width), BF16), shaped((images, both - width), BF16)),
            (core, square, *same, *other),
            [smem] * 2 + [vmem] * plane,
            vmem,
            grant=grant,
        )
        teach, row_lse, col_lse = call(
            logits_kernel,
            (shaped((images, texts), F32), shaped((plane, 2, images), F32), shaped((2, texts), F32)),
            (teacher_scale, student_scale, pupil_text, master_text, pupil_image, master_image),
            [smem, smem] + [vmem] * 4,
            vmem,
            grant=grant,
        )
        row_lse = call(
            join_kernel, shaped((8, images), F32), (exchange(row_lse, PLANE),), [vmem], vmem, flops=MANY
        )
        col_lses = [col_lse] + [to_line(col_lse, s) for s in range(1, depth)]
        image_parts, own_text_part, *text_parts = call(
            functools.partial(weight_kernel, depth),
            (shaped((plane, own, width), BF16), shaped((own, width), F32))
            + (shaped((own, width), BF16),) * (depth - 1),
            (z, student_scale, teach, pupil_image, pupil_text, row_lse, *col_lses),
            [smem] * 2 + [vmem] * (4 + depth),
            vmem,
            (pltpu.VMEM((texts, width), F32),),
            grant,
        )
        out = shaped((own, width), F32)
        image_grad = call(sum_kernel, out, (exchange(image_parts, PLANE),), [vmem], vmem, flops=MANY)
        text_parts = [own_text_part] + [to_line(part, s + 1) for s, part in enumerate(text_parts)]
        return call(
            back_kernel,
            (out, out),
            (image_grad, student_image, student_text, *text_parts),
            [vmem] * (3 + depth),
            vmem,
        )

    return body


def solution(mesh):
    named = physical_mesh(mesh)
    split = P(EVERY, None)
    return jax.shard_map(
        make_body(named.shape["y"] * named.shape["x"], named.shape["z"]),
        mesh=named,
        in_specs=(split, split, split, split, P(), P()),
        out_specs=(split, split),
        check_vma=False,
    )
```

```python
import functools

import jax
import jax.numpy as jnp
from jax import lax
from jax.experimental import pallas as pl
from jax.experimental.pallas import tpu as pltpu
from jax.sharding import Mesh, PartitionSpec as P

EPSILON = 1e-12
SQUARE = ("y", "x")
LINE = "z"
EVERY = ("y", "core", "z", "x")
F32 = jnp.float32
BF16 = jnp.bfloat16
MANY = 1 << 35


def physical_mesh(mesh):
    rows, cols = mesh.shape["row"], mesh.shape["col"]
    side = rows // 2
    wide = side if cols % side == 0 else 1
    return Mesh(mesh.devices.reshape(side, 2, cols // wide, wide), EVERY)


def unit_rows(raw):
    values = raw.astype(F32)
    inverse = lax.rsqrt(jnp.sum(values * values, axis=-1, keepdims=True) + EPSILON)
    return (values * inverse, inverse)


def side_by_side(left, right):
    lowest = jnp.array(-jnp.inf, left.dtype)
    left_width, right_width = left.shape[1], right.shape[1]
    return jnp.maximum(
        lax.pad(left, lowest, ((0, 0, 0), (0, right_width, 0))),
        lax.pad(right, lowest, ((0, 0, 0), (left_width, 0, 0))),
    )


def put_units(block, pupil_ref, master_ref, at):
    own, width = block.shape[0], pupil_ref.shape[1]
    pupil_ref[pl.ds(at, own), :] = unit_rows(block[:, :width])[0].astype(BF16)
    master_ref[pl.ds(at, own), :] = unit_rows(block[:, width:])[0].astype(BF16)


def image_unit_kernel(core_ref, square_ref, *refs):
    pupil_ref, master_ref = refs[-2:]
    blocks = refs[:-2]
    own = blocks[0].shape[0]
    squares = len(blocks) // 2
    core = core_ref[0]
    for s in range(squares):
        at = jnp.bitwise_xor(square_ref[0], s)
        for ref, half in ((blocks[s], core), (blocks[squares + s], 1 - core)):
            row = pl.multiple_of((half * squares + at) * own, own)
            put_units(ref[...], pupil_ref, master_ref, row)


def text_unit_kernel(z_ref, *refs):
    pupil_ref, master_ref = refs[-2:]
    own = refs[0].shape[0]
    for s, ref in enumerate(refs[:-2]):
        row = pl.multiple_of(jnp.bitwise_xor(z_ref[0], s) * own, own)
        put_units(ref[...], pupil_ref, master_ref, row)


def product(left, right):
    return lax.dot_general(left, right, (((1,), (1,)), ((), ())), preferred_element_type=F32)


def block_lse(logits):
    peak = jnp.max(logits, axis=0, keepdims=True)
    return peak + jnp.log(jnp.sum(jnp.exp(logits - peak), axis=0, keepdims=True))


def join_lse(parts):
    top = functools.reduce(jnp.maximum, parts)
    return top + jnp.log(sum(jnp.exp(p - top) for p in parts))


def logits_kernel(
    teacher_scale_ref, student_scale_ref, pupil_text_ref, master_text_ref, pupil_image_ref,
    master_image_ref, teach_ref, rows_ref, cols_ref,
):
    images = pupil_image_ref.shape[0]
    step = min(512, images)
    for k, (scale_ref, image_ref, text_ref) in enumerate(
        (
            (teacher_scale_ref, master_image_ref, master_text_ref),
            (student_scale_ref, pupil_image_ref, pupil_text_ref),
        )
    ):
        scale = scale_ref[0]
        text = text_ref[...]
        columns = []
        for at in range(0, images, step):
            image = image_ref[at : at + step, :]
            logits = scale * product(image, text)
            if k == 0:
                teach_ref[at : at + step, :] = logits
            columns.append(block_lse(logits))
            rows_ref[k : k + 1, at : at + step] = block_lse(scale * product(text, image))
        cols_ref[k : k + 1, :] = join_lse(columns)


def join_kernel(*refs):
    refs[-1][...] = join_lse([ref[...] for ref in refs[:-1]])


def weight_kernel(core_ref, z_ref, scale_ref, teach_ref, image_ref, text_ref, *refs):
    col_ref, row_refs = refs[0], refs[1:3]
    keep_ref, send_ref, own_text_ref = refs[3:6]
    text_out_refs = refs[6:-2]
    image_part_ref, text_part_ref = refs[-2:]
    squares, own, _ = keep_ref.shape
    scale = scale_ref[0]
    images = 2 * squares * own
    step = min(512, images)
    col = col_ref[...]
    rows = join_lse([ref[...] for ref in row_refs])
    rows = jnp.concatenate([rows] * 4, axis=0)
    text = text_ref[...]
    for at in range(0, images, step):
        row = jnp.transpose(rows[:, at : at + step])
        image = image_ref[at : at + step, :]
        teach = teach_ref[at : at + step, :]
        learn = scale * product(image, text)
        rows_part = jnp.exp(learn - row[:, 1:2]) - jnp.exp(teach - row[:, 0:1])
        cols_part = jnp.exp(learn - col[1:2, :]) - jnp.exp(teach - col[0:1, :])
        weight = (0.5 * (rows_part + cols_part)).astype(BF16)
        image_part_ref[at : at + step, :] = scale * jnp.dot(weight, text, preferred_element_type=F32)
        text_part = scale * lax.dot_general(
            weight, image, (((0,), (0,)), ((), ())), preferred_element_type=F32
        )
        if at:
            text_part = text_part_ref[...] + text_part
        text_part_ref[...] = text_part
    core, z = core_ref[0], z_ref[0]
    for i in range(squares):
        for out_ref, half in ((keep_ref, core), (send_ref, 1 - core)):
            row = pl.multiple_of((half * squares + i) * own, own)
            out_ref[i] = image_part_ref[pl.ds(row, own), :].astype(out_ref.dtype)
    own_text_ref[...] = text_part_ref[pl.ds(pl.multiple_of(z * own, own), own), :]
    for s, ref in enumerate(text_out_refs):
        row = pl.multiple_of(jnp.bitwise_xor(z, s + 1) * own, own)
        ref[...] = text_part_ref[pl.ds(row, own), :].astype(BF16)


def back_norm(grad, raw):
    unit, inverse = unit_rows(raw)
    return inverse * (grad - unit * jnp.sum(unit * grad, axis=-1, keepdims=True))


def pair_kernel(square_ref, kept_ref, received_ref, *refs):
    for s, ref in enumerate(refs):
        at = jnp.bitwise_xor(square_ref[0], s)
        ref[...] = (kept_ref[at] + received_ref[at].astype(F32)).astype(ref.dtype)


def total_of(refs):
    total = refs[0][...]
    for ref in refs[1:]:
        total = total + ref[...].astype(F32)
    return total


def sum_kernel(*refs):
    refs[-1][...] = total_of(refs[:-1])


def back_kernel(raw_image_ref, raw_text_ref, text_ref, *refs):
    image_out_ref, text_out_ref = refs[-2:]
    text_out_ref[...] = back_norm(text_ref[...], raw_text_ref[...])
    image_out_ref[...] = back_norm(total_of(refs[:-2]), raw_image_ref[...])


def shaped(shape, dtype):
    return jax.ShapeDtypeStruct(shape, dtype)


def call(kernel, outs, ins, specs, out_spec, scratch=(), grant=16, flops=1 << 20):
    return pl.pallas_call(
        kernel,
        out_shape=outs,
        in_specs=specs,
        out_specs=jax.tree.map(lambda _: out_spec, outs),
        scratch_shapes=list(scratch),
        compiler_params=pltpu.CompilerParams(vmem_limit_bytes=grant << 20),
        cost_estimate=pl.CostEstimate(flops=flops, bytes_accessed=1 << 20, transcendentals=0),
    )(*ins)


def bits(count):
    return [1 << i for i in reversed(range((count - 1).bit_length()))]


def make_body(squares, depth):
    plane = 2 * squares
    vmem = pl.BlockSpec(memory_space=pltpu.VMEM)
    smem = pl.BlockSpec(memory_space=pltpu.SMEM)

    def to_line(value, step):
        return lax.ppermute(value, LINE, [(z, z ^ step) for z in range(depth)])

    def to_square(value, step):
        return lax.ppermute(value, SQUARE, [(q, q ^ step) for q in range(squares)])

    def gather_line(value):
        first = bits(depth)
        held = lax.optimization_barrier([value] + [to_line(value, s) for s in first])
        blocks = dict(zip([0] + first, held))
        for s in sorted(set(range(depth)) - set(blocks), key=lambda s: bin(s).count("1")):
            near = s & -s
            blocks[s] = to_line(blocks[s ^ near], near)
        return [blocks[s] for s in range(depth)]

    def to_sibling(value):
        return lax.ppermute(value, "core", [(0, 1), (1, 0)])

    def body(student_image, student_text, teacher_image, teacher_text, teacher_scale, student_scale):
        own, width = student_image.shape
        both = width + teacher_image.shape[1]
        images, texts = plane * own, depth * own
        core = lax.axis_index("core").astype(jnp.int32).reshape(1)
        square = lax.axis_index("y") * lax.axis_size("x") + lax.axis_index("x")
        square = square.astype(jnp.int32).reshape(1)
        z = lax.axis_index("z").astype(jnp.int32).reshape(1)
        teacher_scale = teacher_scale.reshape(1)
        student_scale = student_scale.reshape(1)
        grant = 16 if images * texts <= 512 * 256 else 56

        raw_text = side_by_side(student_text, teacher_text)
        raw_texts = gather_line(raw_text)
        raw_image = side_by_side(student_image, teacher_image)
        same = [raw_image] + [to_square(raw_image, s) for s in range(1, squares)]
        other = [to_sibling(block) for block in same]

        pupil_text, master_text = call(
            text_unit_kernel,
            (shaped((texts, width), BF16), shaped((texts, both - width), BF16)),
            (z, *raw_texts),
            [smem] + [vmem] * depth,
            vmem,
            grant=grant,
            flops=MANY,
        )
        pupil_image, master_image = call(
            image_unit_kernel,
            (shaped((images, width), BF16), shaped((images, both - width), BF16)),
            (core, square, *same, *other),
            [smem] * 2 + [vmem] * plane,
            vmem,
            grant=grant,
        )
        teach, row_lse, col_lse = call(
            logits_kernel,
            (shaped((images, texts), F32), shaped((2, images), F32), shaped((2, texts), F32)),
            (teacher_scale, student_scale, pupil_text, master_text, pupil_image, master_image),
            [smem, smem] + [vmem] * 4,
            vmem,
            grant=grant,
        )
        def joined(parts, flops):
            out = shaped(parts[0].shape, F32)
            return call(join_kernel, out, parts, [vmem] * 2, vmem, flops=flops)

        row_lses = [row_lse, to_sibling(row_lse)]
        for s in reversed(bits(squares)):
            row_lse = joined(row_lses, 1 << 10)
            row_lses = [row_lse, to_square(row_lse, s)]
        for s in bits(depth):
            col_lse = joined([col_lse, to_line(col_lse, s)], MANY if s == 1 else 1 << 31)
        block = shaped((own, width), F32)
        sent = shaped((own, width), BF16)
        kept, for_sibling, own_text, *for_line = call(
            weight_kernel,
            (shaped((squares, own, width), F32), shaped((squares, own, width), BF16), block)
            + (sent,) * (depth - 1),
            (core, z, student_scale, teach, pupil_image, pupil_text, col_lse, *row_lses),
            [smem] * 3 + [vmem] * 6,
            vmem,
            (pltpu.VMEM((images, width), F32), pltpu.VMEM((texts, width), F32)),
            grant,
        )
        text_parts = [own_text] + [to_line(part, s + 1) for s, part in enumerate(for_line)]
        text_grad = call(sum_kernel, block, text_parts, [vmem] * depth, vmem, flops=MANY)
        own_image, *for_square = call(
            pair_kernel,
            (block,) + (sent,) * (squares - 1),
            (square, kept, to_sibling(for_sibling)),
            [smem] + [vmem] * 2,
            vmem,
        )
        image_parts = [own_image] + [to_square(part, s + 1) for s, part in enumerate(for_square)]
        return call(
            back_kernel,
            (block, block),
            (student_image, student_text, text_grad, *image_parts),
            [vmem] * (3 + squares),
            vmem,
        )

    return body


def solution(mesh):
    named = physical_mesh(mesh)
    split = P(EVERY, None)
    return jax.shard_map(
        make_body(named.shape["y"] * named.shape["x"], named.shape["z"]),
        mesh=named,
        in_specs=(split, split, split, split, P(), P()),
        out_specs=(split, split),
        check_vma=False,
    )
```

```python
import functools

import jax
import jax.numpy as jnp
from jax import lax
from jax.experimental import pallas as pl
from jax.experimental.pallas import tpu as pltpu
from jax.sharding import Mesh, PartitionSpec as P

EPSILON = 1e-12
SQUARE = ("y", "x")
LINE = "z"
EVERY = ("y", "core", "z", "x")
F32 = jnp.float32
BF16 = jnp.bfloat16
MANY = 1 << 35


def physical_mesh(mesh):
    rows, cols = mesh.shape["row"], mesh.shape["col"]
    side = rows // 2
    wide = side if cols % side == 0 else 1
    return Mesh(mesh.devices.reshape(side, 2, cols // wide, wide), EVERY)


def unit_rows(raw):
    values = raw.astype(F32)
    inverse = lax.rsqrt(jnp.sum(values * values, axis=-1, keepdims=True) + EPSILON)
    return (values * inverse, inverse)


def side_by_side(left, right):
    lowest = jnp.array(-jnp.inf, left.dtype)
    left_width, right_width = left.shape[1], right.shape[1]
    return jnp.maximum(
        lax.pad(left, lowest, ((0, 0, 0), (0, right_width, 0))),
        lax.pad(right, lowest, ((0, 0, 0), (left_width, 0, 0))),
    )


def put_units(block, pupil_ref, master_ref, at):
    own, width = block.shape[0], pupil_ref.shape[1]
    pupil_ref[pl.ds(at, own), :] = unit_rows(block[:, :width])[0].astype(BF16)
    master_ref[pl.ds(at, own), :] = unit_rows(block[:, width:])[0].astype(BF16)


def image_unit_kernel(core_ref, square_ref, *refs):
    pupil_ref, master_ref = refs[-2:]
    blocks = refs[:-2]
    own = blocks[0].shape[0]
    squares = len(blocks) // 2
    core = core_ref[0]
    for s in range(squares):
        at = jnp.bitwise_xor(square_ref[0], squares - 1 - s)
        for ref, half in ((blocks[s], core), (blocks[squares + s], 1 - core)):
            row = pl.multiple_of((half * squares + at) * own, own)
            put_units(ref[...], pupil_ref, master_ref, row)


def text_unit_kernel(z_ref, *refs):
    pupil_ref, master_ref = refs[-2:]
    own = refs[0].shape[0]
    for s, ref in enumerate(refs[:-2]):
        row = pl.multiple_of(jnp.bitwise_xor(z_ref[0], s) * own, own)
        put_units(ref[...], pupil_ref, master_ref, row)


def product(left, right):
    return lax.dot_general(left, right, (((1,), (1,)), ((), ())), preferred_element_type=F32)


def block_lse(logits):
    peak = jnp.max(logits, axis=0, keepdims=True)
    return peak + jnp.log(jnp.sum(jnp.exp(logits - peak), axis=0, keepdims=True))


def join_lse(parts):
    top = functools.reduce(jnp.maximum, parts)
    return top + jnp.log(sum(jnp.exp(p - top) for p in parts))


def logits_kernel(
    teacher_scale_ref, student_scale_ref, pupil_text_ref, master_text_ref, pupil_image_ref,
    master_image_ref, teach_ref, rows_ref, cols_ref,
):
    images = pupil_image_ref.shape[0]
    step = min(512, images)
    for k, (scale_ref, image_ref, text_ref) in enumerate(
        (
            (teacher_scale_ref, master_image_ref, master_text_ref),
            (student_scale_ref, pupil_image_ref, pupil_text_ref),
        )
    ):
        scale = scale_ref[0]
        text = text_ref[...]
        columns = []
        for at in range(0, images, step):
            image = image_ref[at : at + step, :]
            logits = scale * product(image, text)
            if k == 0:
                teach_ref[at : at + step, :] = logits
            columns.append(block_lse(logits))
            rows_ref[k : k + 1, at : at + step] = block_lse(scale * product(text, image))
        cols_ref[k : k + 1, :] = join_lse(columns)


def join_kernel(*refs):
    refs[-1][...] = join_lse([ref[...] for ref in refs[:-1]])


def weight_kernel(core_ref, z_ref, scale_ref, teach_ref, image_ref, text_ref, *refs):
    col_ref, row_refs = refs[0], refs[1:3]
    keep_ref, send_ref, own_text_ref = refs[3:6]
    text_out_refs = refs[6:-2]
    image_part_ref, text_part_ref = refs[-2:]
    squares, own, _ = keep_ref.shape
    scale = scale_ref[0]
    images = 2 * squares * own
    step = min(512, images)
    col = col_ref[...]
    rows = join_lse([ref[...] for ref in row_refs])
    rows = jnp.concatenate([rows] * 4, axis=0)
    text = text_ref[...]
    for at in range(0, images, step):
        row = jnp.transpose(rows[:, at : at + step])
        image = image_ref[at : at + step, :]
        teach = teach_ref[at : at + step, :]
        learn = scale * product(image, text)
        rows_part = jnp.exp(learn - row[:, 1:2]) - jnp.exp(teach - row[:, 0:1])
        cols_part = jnp.exp(learn - col[1:2, :]) - jnp.exp(teach - col[0:1, :])
        weight = (0.5 * (rows_part + cols_part)).astype(BF16)
        image_part_ref[at : at + step, :] = scale * jnp.dot(weight, text, preferred_element_type=F32)
        text_part = scale * lax.dot_general(
            weight, image, (((0,), (0,)), ((), ())), preferred_element_type=F32
        )
        if at:
            text_part = text_part_ref[...] + text_part
        text_part_ref[...] = text_part
    core, z = core_ref[0], z_ref[0]
    for i in range(squares):
        for out_ref, half in ((keep_ref, core), (send_ref, 1 - core)):
            row = pl.multiple_of((half * squares + i) * own, own)
            out_ref[i] = image_part_ref[pl.ds(row, own), :].astype(out_ref.dtype)
    own_text_ref[...] = text_part_ref[pl.ds(pl.multiple_of(z * own, own), own), :]
    for s, ref in enumerate(text_out_refs):
        row = pl.multiple_of(jnp.bitwise_xor(z, s + 1) * own, own)
        ref[...] = text_part_ref[pl.ds(row, own), :].astype(BF16)


def back_norm(grad, raw):
    unit, inverse = unit_rows(raw)
    return inverse * (grad - unit * jnp.sum(unit * grad, axis=-1, keepdims=True))


def pair_kernel(square_ref, kept_ref, received_ref, *refs):
    for s, ref in enumerate(refs):
        at = jnp.bitwise_xor(square_ref[0], s)
        ref[...] = (kept_ref[at] + received_ref[at].astype(F32)).astype(ref.dtype)


def back_kernel(raw_ref, own_ref, *refs):
    grad = own_ref[...]
    for ref in refs[:-1]:
        grad = grad + ref[...].astype(F32)
    refs[-1][...] = back_norm(grad, raw_ref[...])


def shaped(shape, dtype):
    return jax.ShapeDtypeStruct(shape, dtype)


def call(kernel, outs, ins, specs, out_spec, scratch=(), grant=16, flops=1 << 20):
    return pl.pallas_call(
        kernel,
        out_shape=outs,
        in_specs=specs,
        out_specs=jax.tree.map(lambda _: out_spec, outs),
        scratch_shapes=list(scratch),
        compiler_params=pltpu.CompilerParams(vmem_limit_bytes=grant << 20),
        cost_estimate=pl.CostEstimate(flops=flops, bytes_accessed=1 << 20, transcendentals=0),
    )(*ins)


def bits(count):
    return [1 << i for i in reversed(range((count - 1).bit_length()))]


def make_body(squares, depth):
    plane = 2 * squares
    vmem = pl.BlockSpec(memory_space=pltpu.VMEM)
    smem = pl.BlockSpec(memory_space=pltpu.SMEM)

    def to_line(value, step):
        return lax.ppermute(value, LINE, [(z, z ^ step) for z in range(depth)])

    def to_square(value, step):
        return lax.ppermute(value, SQUARE, [(q, q ^ step) for q in range(squares)])

    def gather_line(value):
        first = bits(depth)
        held = lax.optimization_barrier([value] + [to_line(value, s) for s in first])
        blocks = dict(zip([0] + first, held))
        for s in sorted(set(range(depth)) - set(blocks), key=lambda s: bin(s).count("1")):
            near = s & -s
            blocks[s] = to_line(blocks[s ^ near], near)
        return [blocks[s] for s in range(depth)]

    def to_sibling(value):
        return lax.ppermute(value, "core", [(0, 1), (1, 0)])

    def body(student_image, student_text, teacher_image, teacher_text, teacher_scale, student_scale):
        own, width = student_image.shape
        both = width + teacher_image.shape[1]
        images, texts = plane * own, depth * own
        core = lax.axis_index("core").astype(jnp.int32).reshape(1)
        square = lax.axis_index("y") * lax.axis_size("x") + lax.axis_index("x")
        square = square.astype(jnp.int32).reshape(1)
        z = lax.axis_index("z").astype(jnp.int32).reshape(1)
        teacher_scale = teacher_scale.reshape(1)
        student_scale = student_scale.reshape(1)
        grant = 16 if images * texts <= 512 * 256 else 56

        raw_text = side_by_side(student_text, teacher_text)
        raw_texts = gather_line(raw_text)
        raw_image = side_by_side(student_image, teacher_image)
        same = [to_square(raw_image, s) for s in reversed(range(1, squares))] + [raw_image]
        other = [to_sibling(block) for block in same]

        pupil_text, master_text = call(
            text_unit_kernel,
            (shaped((texts, width), BF16), shaped((texts, both - width), BF16)),
            (z, *raw_texts),
            [smem] + [vmem] * depth,
            vmem,
            grant=grant,
            flops=MANY,
        )
        pupil_image, master_image = call(
            image_unit_kernel,
            (shaped((images, width), BF16), shaped((images, both - width), BF16)),
            (core, square, *same, *other),
            [smem] * 2 + [vmem] * plane,
            vmem,
            grant=grant,
        )
        teach, row_lse, col_lse = call(
            logits_kernel,
            (shaped((images, texts), F32), shaped((2, images), F32), shaped((2, texts), F32)),
            (teacher_scale, student_scale, pupil_text, master_text, pupil_image, master_image),
            [smem, smem] + [vmem] * 4,
            vmem,
            grant=grant,
        )
        def joined(parts, flops):
            out = shaped(parts[0].shape, F32)
            return call(join_kernel, out, parts, [vmem] * 2, vmem, flops=flops)

        row_lses = [row_lse, to_sibling(row_lse)]
        for s in reversed(bits(squares)):
            row_lse = joined(row_lses, 1 << 10)
            row_lses = [row_lse, to_square(row_lse, s)]
        for s in bits(depth):
            col_lse = joined([col_lse, to_line(col_lse, s)], MANY if s == 1 else 1 << 10)
        block = shaped((own, width), F32)
        sent = shaped((own, width), BF16)
        kept, for_sibling, own_text, *for_line = call(
            weight_kernel,
            (shaped((squares, own, width), F32), shaped((squares, own, width), BF16), block)
            + (sent,) * (depth - 1),
            (core, z, student_scale, teach, pupil_image, pupil_text, col_lse, *row_lses),
            [smem] * 3 + [vmem] * 6,
            vmem,
            (pltpu.VMEM((images, width), F32), pltpu.VMEM((texts, width), F32)),
            grant,
        )
        text_parts = [to_line(part, s + 1) for s, part in reversed(list(enumerate(for_line)))]
        text_grad = call(
            back_kernel,
            block,
            (student_text, own_text, *text_parts),
            [vmem] * (1 + depth),
            vmem,
            flops=MANY,
        )
        own_image, *for_square = call(
            pair_kernel,
            (block,) + (sent,) * (squares - 1),
            (square, kept, to_sibling(for_sibling)),
            [smem] + [vmem] * 2,
            vmem,
        )
        image_parts = [to_square(part, s + 1) for s, part in reversed(list(enumerate(for_square)))]
        image_grad = call(
            back_kernel,
            block,
            (student_image, own_image, *image_parts),
            [vmem] * (1 + squares),
            vmem,
        )
        return (image_grad, text_grad)

    return body


def solution(mesh):
    named = physical_mesh(mesh)
    split = P(EVERY, None)
    return jax.shard_map(
        make_body(named.shape["y"] * named.shape["x"], named.shape["z"]),
        mesh=named,
        in_specs=(split, split, split, split, P(), P()),
        out_specs=(split, split),
        check_vma=False,
    )
```

```python
import functools

import jax
import jax.numpy as jnp
from jax import lax
from jax.experimental import pallas as pl
from jax.experimental.pallas import tpu as pltpu
from jax.sharding import Mesh, PartitionSpec as P

EPSILON = 1e-12
SQUARE = ("y", "x")
LINE = "z"
EVERY = ("y", "core", "z", "x")
F32 = jnp.float32
BF16 = jnp.bfloat16
FEW, SOME, MANY = 1 << 10, 1 << 31, 1 << 35


def physical_mesh(mesh):
    rows, cols = mesh.shape["row"], mesh.shape["col"]
    side = rows // 2
    wide = side if cols % side == 0 else 1
    return Mesh(mesh.devices.reshape(side, 2, cols // wide, wide), EVERY)


def unit_rows(raw):
    values = raw.astype(F32)
    inverse = lax.rsqrt(jnp.sum(values * values, axis=-1, keepdims=True) + EPSILON)
    return (values * inverse, inverse)


def side_by_side(left, right):
    lowest = jnp.array(-jnp.inf, left.dtype)
    left_width, right_width = left.shape[1], right.shape[1]
    return jnp.maximum(
        lax.pad(left, lowest, ((0, 0, 0), (0, right_width, 0))),
        lax.pad(right, lowest, ((0, 0, 0), (left_width, 0, 0))),
    )


def put_units(block, pupil_ref, master_ref, at):
    own, width = block.shape[0], pupil_ref.shape[1]
    pupil_ref[pl.ds(at, own), :] = unit_rows(block[:, :width])[0].astype(BF16)
    master_ref[pl.ds(at, own), :] = unit_rows(block[:, width:])[0].astype(BF16)


def image_unit_kernel(core_ref, square_ref, *refs):
    pupil_ref, master_ref = refs[-2:]
    blocks = refs[:-2]
    own = blocks[0].shape[0]
    squares = len(blocks) // 2
    core = core_ref[0]
    for s in range(squares):
        at = jnp.bitwise_xor(square_ref[0], squares - 1 - s)
        for ref, half in ((blocks[s], core), (blocks[squares + s], 1 - core)):
            row = pl.multiple_of((half * squares + at) * own, own)
            put_units(ref[...], pupil_ref, master_ref, row)


def text_unit_kernel(z_ref, *refs):
    pupil_ref, master_ref = refs[-2:]
    own = refs[0].shape[0]
    for s, ref in enumerate(refs[:-2]):
        row = pl.multiple_of(jnp.bitwise_xor(z_ref[0], s) * own, own)
        put_units(ref[...], pupil_ref, master_ref, row)


def product(left, right):
    return lax.dot_general(left, right, (((1,), (1,)), ((), ())), preferred_element_type=F32)


def block_lse(logits):
    peak = jnp.max(logits, axis=0, keepdims=True)
    return peak + jnp.log(jnp.sum(jnp.exp(logits - peak), axis=0, keepdims=True))


def join_lse(parts):
    top = functools.reduce(jnp.maximum, parts)
    return top + jnp.log(sum(jnp.exp(p - top) for p in parts))


def logits_kernel(
    teacher_scale_ref, student_scale_ref, pupil_text_ref, master_text_ref, pupil_image_ref,
    master_image_ref, teach_ref, rows_ref, cols_ref,
):
    images = pupil_image_ref.shape[0]
    step = min(512, images)
    for k, (scale_ref, image_ref, text_ref) in enumerate(
        (
            (teacher_scale_ref, master_image_ref, master_text_ref),
            (student_scale_ref, pupil_image_ref, pupil_text_ref),
        )
    ):
        scale = scale_ref[0]
        text = text_ref[...]
        columns = []
        for at in range(0, images, step):
            image = image_ref[at : at + step, :]
            logits = scale * product(image, text)
            if k == 0:
                teach_ref[at : at + step, :] = logits
            columns.append(block_lse(logits))
            rows_ref[k : k + 1, at : at + step] = block_lse(scale * product(text, image))
        cols_ref[k : k + 1, :] = join_lse(columns)


def join_kernel(*refs):
    refs[-1][...] = join_lse([ref[...] for ref in refs[:-1]])


def weight_kernel(core_ref, z_ref, scale_ref, teach_ref, image_ref, text_ref, *refs):
    col_ref, row_ref, keep_ref, send_ref, own_text_ref = refs[:5]
    text_out_refs = refs[5:-2]
    image_part_ref, text_part_ref = refs[-2:]
    squares, own, _ = keep_ref.shape
    scale = scale_ref[0]
    images = 2 * squares * own
    step = min(512, images)
    col = col_ref[...]
    rows = jnp.concatenate([row_ref[...]] * 4, axis=0)
    text = text_ref[...]
    for at in range(0, images, step):
        row = jnp.transpose(rows[:, at : at + step])
        image = image_ref[at : at + step, :]
        teach = teach_ref[at : at + step, :]
        learn = scale * product(image, text)
        rows_part = jnp.exp(learn - row[:, 1:2]) - jnp.exp(teach - row[:, 0:1])
        cols_part = jnp.exp(learn - col[1:2, :]) - jnp.exp(teach - col[0:1, :])
        weight = (0.5 * (rows_part + cols_part)).astype(BF16)
        image_part_ref[at : at + step, :] = scale * jnp.dot(weight, text, preferred_element_type=F32)
        text_part = scale * lax.dot_general(
            weight, image, (((0,), (0,)), ((), ())), preferred_element_type=F32
        )
        if at:
            text_part = text_part_ref[...] + text_part
        text_part_ref[...] = text_part
    core, z = core_ref[0], z_ref[0]
    for i in range(squares):
        for out_ref, half in ((keep_ref, core), (send_ref, 1 - core)):
            row = pl.multiple_of((half * squares + i) * own, own)
            out_ref[i] = image_part_ref[pl.ds(row, own), :].astype(out_ref.dtype)
    own_text_ref[...] = text_part_ref[pl.ds(pl.multiple_of(z * own, own), own), :]
    for s, ref in enumerate(text_out_refs):
        row = pl.multiple_of(jnp.bitwise_xor(z, s + 1) * own, own)
        ref[...] = text_part_ref[pl.ds(row, own), :].astype(BF16)


def back_norm(grad, raw):
    unit, inverse = unit_rows(raw)
    return inverse * (grad - unit * jnp.sum(unit * grad, axis=-1, keepdims=True))


def pair_kernel(square_ref, kept_ref, received_ref, *refs):
    for s, ref in enumerate(refs):
        at = jnp.bitwise_xor(square_ref[0], s)
        ref[...] = (kept_ref[at] + received_ref[at].astype(F32)).astype(ref.dtype)


def total_of(refs):
    total = refs[0][...]
    for ref in refs[1:]:
        total = total + ref[...].astype(F32)
    return total


def sum_kernel(*refs):
    refs[-1][...] = total_of(refs[:-1])


def back_kernel(raw_image_ref, raw_text_ref, text_ref, *refs):
    image_out_ref, text_out_ref = refs[-2:]
    text_out_ref[...] = back_norm(text_ref[...], raw_text_ref[...])
    image_out_ref[...] = back_norm(total_of(refs[:-2]), raw_image_ref[...])


def shaped(shape, dtype):
    return jax.ShapeDtypeStruct(shape, dtype)


def call(kernel, outs, ins, specs, out_spec, scratch=(), grant=16, flops=1 << 20):
    return pl.pallas_call(
        kernel,
        out_shape=outs,
        in_specs=specs,
        out_specs=jax.tree.map(lambda _: out_spec, outs),
        scratch_shapes=list(scratch),
        compiler_params=pltpu.CompilerParams(vmem_limit_bytes=grant << 20),
        cost_estimate=pl.CostEstimate(flops=flops, bytes_accessed=1 << 20, transcendentals=0),
    )(*ins)


def bits(count):
    return [1 << i for i in reversed(range((count - 1).bit_length()))]


def make_body(squares, depth):
    plane = 2 * squares
    vmem = pl.BlockSpec(memory_space=pltpu.VMEM)
    smem = pl.BlockSpec(memory_space=pltpu.SMEM)

    def to_line(value, step):
        return lax.ppermute(value, LINE, [(z, z ^ step) for z in range(depth)])

    def to_square(value, step):
        return lax.ppermute(value, SQUARE, [(q, q ^ step) for q in range(squares)])

    def gather_line(value):
        first = bits(depth)
        held = lax.optimization_barrier([value] + [to_line(value, s) for s in first])
        blocks = dict(zip([0] + first, held))
        for s in sorted(set(range(depth)) - set(blocks), key=lambda s: bin(s).count("1")):
            near = s & -s
            blocks[s] = to_line(blocks[s ^ near], near)
        return [blocks[s] for s in range(depth)]

    def to_sibling(value):
        return lax.ppermute(value, "core", [(0, 1), (1, 0)])

    def body(student_image, student_text, teacher_image, teacher_text, teacher_scale, student_scale):
        own, width = student_image.shape
        both = width + teacher_image.shape[1]
        images, texts = plane * own, depth * own
        core = lax.axis_index("core").astype(jnp.int32).reshape(1)
        square = lax.axis_index("y") * lax.axis_size("x") + lax.axis_index("x")
        square = square.astype(jnp.int32).reshape(1)
        z = lax.axis_index("z").astype(jnp.int32).reshape(1)
        teacher_scale = teacher_scale.reshape(1)
        student_scale = student_scale.reshape(1)
        grant = 16 if images * texts <= 512 * 256 else 56

        raw_text = side_by_side(student_text, teacher_text)
        raw_texts = gather_line(raw_text)
        raw_image = side_by_side(student_image, teacher_image)
        same = [to_square(raw_image, s) for s in reversed(range(1, squares))] + [raw_image]
        other = [to_sibling(block) for block in same]

        pupil_text, master_text = call(
            text_unit_kernel,
            (shaped((texts, width), BF16), shaped((texts, both - width), BF16)),
            (z, *raw_texts),
            [smem] + [vmem] * depth,
            vmem,
            grant=grant,
            flops=MANY,
        )
        pupil_image, master_image = call(
            image_unit_kernel,
            (shaped((images, width), BF16), shaped((images, both - width), BF16)),
            (core, square, *same, *other),
            [smem] * 2 + [vmem] * plane,
            vmem,
            grant=grant,
        )
        teach, row_lse, col_lse = call(
            logits_kernel,
            (shaped((images, texts), F32), shaped((2, images), F32), shaped((2, texts), F32)),
            (teacher_scale, student_scale, pupil_text, master_text, pupil_image, master_image),
            [smem, smem] + [vmem] * 4,
            vmem,
            grant=grant,
        )
        def joined(parts, flops):
            out = shaped(parts[0].shape, F32)
            return call(join_kernel, out, parts, [vmem] * len(parts), vmem, flops=flops)

        row_lse = joined([row_lse, to_sibling(row_lse)], FEW)
        row_lses = [to_square(row_lse, s) for s in reversed(range(1, squares))]
        row_lse = joined([row_lse, *row_lses], MANY)
        for s in bits(depth):
            col_lse = joined([col_lse, to_line(col_lse, s)], FEW if s == 1 else SOME)
        block = shaped((own, width), F32)
        sent = shaped((own, width), BF16)
        kept, for_sibling, own_text, *for_line = call(
            weight_kernel,
            (shaped((squares, own, width), F32), shaped((squares, own, width), BF16), block)
            + (sent,) * (depth - 1),
            (core, z, student_scale, teach, pupil_image, pupil_text, col_lse, row_lse),
            [smem] * 3 + [vmem] * 5,
            vmem,
            (pltpu.VMEM((images, width), F32), pltpu.VMEM((texts, width), F32)),
            grant,
        )
        text_parts = [to_line(part, s + 1) for s, part in enumerate(for_line)]
        text_grad = call(sum_kernel, block, (own_text, *text_parts), [vmem] * depth, vmem, flops=MANY)
        own_image, *for_square = call(
            pair_kernel,
            (block,) + (sent,) * (squares - 1),
            (square, kept, to_sibling(for_sibling)),
            [smem] + [vmem] * 2,
            vmem,
        )
        image_parts = [to_square(part, s + 1) for s, part in reversed(list(enumerate(for_square)))]
        return call(
            back_kernel,
            (block, block),
            (student_image, student_text, text_grad, own_image, *image_parts),
            [vmem] * (3 + squares),
            vmem,
        )

    return body


def solution(mesh):
    named = physical_mesh(mesh)
    split = P(EVERY, None)
    return jax.shard_map(
        make_body(named.shape["y"] * named.shape["x"], named.shape["z"]),
        mesh=named,
        in_specs=(split, split, split, split, P(), P()),
        out_specs=(split, split),
        check_vma=False,
    )
```

```python
import functools

import jax
import jax.numpy as jnp
from jax import lax
from jax.experimental import pallas as pl
from jax.experimental.pallas import tpu as pltpu
from jax.sharding import Mesh, PartitionSpec as P

EPSILON = 1e-12
SQUARE = ("y", "x")
LINE = "z"
EVERY = ("y", "core", "z", "x")
F32 = jnp.float32
BF16 = jnp.bfloat16
FEW, SOME, MANY = 1 << 10, 1 << 31, 1 << 35


def physical_mesh(mesh):
    rows, cols = mesh.shape["row"], mesh.shape["col"]
    side = rows // 2
    wide = side if cols % side == 0 else 1
    return Mesh(mesh.devices.reshape(side, 2, cols // wide, wide), EVERY)


def unit_rows(raw):
    values = raw.astype(F32)
    inverse = lax.rsqrt(jnp.sum(values * values, axis=-1, keepdims=True) + EPSILON)
    return (values * inverse, inverse)


def side_by_side(left, right):
    lowest = jnp.array(-jnp.inf, left.dtype)
    left_width, right_width = left.shape[1], right.shape[1]
    return jnp.maximum(
        lax.pad(left, lowest, ((0, 0, 0), (0, right_width, 0))),
        lax.pad(right, lowest, ((0, 0, 0), (left_width, 0, 0))),
    )


def put_units(block, pupil_ref, master_ref, at):
    own, width = block.shape[0], pupil_ref.shape[1]
    pupil_ref[pl.ds(at, own), :] = unit_rows(block[:, :width])[0].astype(BF16)
    master_ref[pl.ds(at, own), :] = unit_rows(block[:, width:])[0].astype(BF16)


def image_unit_kernel(square_ref, *refs):
    pupil_ref, master_ref = refs[-2:]
    own = refs[0].shape[0]
    for s, ref in enumerate(refs[:-2]):
        row = pl.multiple_of(jnp.bitwise_xor(square_ref[0], s) * own, own)
        put_units(ref[...], pupil_ref, master_ref, row)


def text_unit_kernel(z_ref, *refs):
    pupil_ref, master_ref = refs[-2:]
    own = refs[0].shape[0]
    for s, ref in enumerate(refs[:-2]):
        row = pl.multiple_of(jnp.bitwise_xor(z_ref[0], s) * own, own)
        put_units(ref[...], pupil_ref, master_ref, row)


def product(left, right):
    return lax.dot_general(left, right, (((1,), (1,)), ((), ())), preferred_element_type=F32)


def block_lse(logits):
    peak = jnp.max(logits, axis=0, keepdims=True)
    return peak + jnp.log(jnp.sum(jnp.exp(logits - peak), axis=0, keepdims=True))


def join_lse(parts):
    top = functools.reduce(jnp.maximum, parts)
    return top + jnp.log(sum(jnp.exp(p - top) for p in parts))


def chunks(pairs):
    half = pairs[0][0].shape[0]
    step = min(512, half)
    return [
        (k * half + at, [pair[k] for pair in pairs], slice(at, at + step))
        for k in range(2)
        for at in range(0, half, step)
    ]


def logits_kernel(
    teacher_scale_ref, student_scale_ref, pupil_text_ref, master_text_ref, pupil_same_ref,
    pupil_other_ref, master_same_ref, master_other_ref, teach_ref, rows_ref, cols_ref,
):
    for k, (scale_ref, pair, text_ref) in enumerate(
        (
            (teacher_scale_ref, (master_same_ref, master_other_ref), master_text_ref),
            (student_scale_ref, (pupil_same_ref, pupil_other_ref), pupil_text_ref),
        )
    ):
        scale = scale_ref[0]
        text = text_ref[...]
        columns = []
        for at, (ref,), part in chunks([pair]):
            image = ref[part, :]
            rows = slice(at, at + image.shape[0])
            logits = scale * product(image, text)
            if k == 0:
                teach_ref[rows, :] = logits
            columns.append(block_lse(logits))
            rows_ref[k : k + 1, rows] = block_lse(scale * product(text, image))
        cols_ref[k : k + 1, :] = join_lse(columns)


def join_kernel(*refs):
    refs[-1][...] = join_lse([ref[...] for ref in refs[:-1]])


def join_sibling_kernel(own_ref, other_ref, out_ref):
    half = own_ref.shape[1] // 2
    for here, there in ((slice(0, half), slice(half, None)), (slice(half, None), slice(0, half))):
        out_ref[:, here] = join_lse([own_ref[:, here], other_ref[:, there]])


def weight_kernel(z_ref, scale_ref, teach_ref, same_ref, other_ref, text_ref, col_ref, row_ref, *refs):
    keep_ref, send_ref, own_text_ref = refs[:3]
    text_out_refs = refs[3:-1]
    text_part_ref = refs[-1]
    squares, own, width = keep_ref.shape
    scale = scale_ref[0]
    col = col_ref[...]
    rows = jnp.concatenate([row_ref[...]] * 4, axis=0)
    text = text_ref[...]
    pairs = [(same_ref, other_ref), (keep_ref, send_ref)]
    pairs[1] = tuple(ref.reshape(squares * own, width) for ref in pairs[1])
    text_part = None
    for at, (image_ref, out_ref), part in chunks(pairs):
        image = image_ref[part, :]
        here = slice(at, at + image.shape[0])
        row = jnp.transpose(rows[:, here])
        teach = teach_ref[here, :]
        learn = scale * product(image, text)
        rows_part = jnp.exp(learn - row[:, 1:2]) - jnp.exp(teach - row[:, 0:1])
        cols_part = jnp.exp(learn - col[1:2, :]) - jnp.exp(teach - col[0:1, :])
        weight = (0.5 * (rows_part + cols_part)).astype(BF16)
        image_part = scale * jnp.dot(weight, text, preferred_element_type=F32)
        out_ref[part, :] = image_part.astype(out_ref.dtype)
        piece = scale * lax.dot_general(
            weight, image, (((0,), (0,)), ((), ())), preferred_element_type=F32
        )
        text_part = piece if text_part is None else text_part + piece
    text_part_ref[...] = text_part
    z = z_ref[0]
    own_text_ref[...] = text_part_ref[pl.ds(pl.multiple_of(z * own, own), own), :]
    for s, ref in enumerate(text_out_refs):
        row = pl.multiple_of(jnp.bitwise_xor(z, s + 1) * own, own)
        ref[...] = text_part_ref[pl.ds(row, own), :].astype(BF16)


def back_norm(grad, raw):
    unit, inverse = unit_rows(raw)
    return inverse * (grad - unit * jnp.sum(unit * grad, axis=-1, keepdims=True))


def pair_kernel(square_ref, kept_ref, received_ref, *refs):
    for s, ref in enumerate(refs):
        at = jnp.bitwise_xor(square_ref[0], s)
        ref[...] = (kept_ref[at] + received_ref[at].astype(F32)).astype(ref.dtype)


def total_of(refs):
    total = refs[0][...]
    for ref in refs[1:]:
        total = total + ref[...].astype(F32)
    return total


def sum_kernel(*refs):
    refs[-1][...] = total_of(refs[:-1])


def back_kernel(raw_image_ref, raw_text_ref, text_ref, *refs):
    image_out_ref, text_out_ref = refs[-2:]
    text_out_ref[...] = back_norm(text_ref[...], raw_text_ref[...])
    image_out_ref[...] = back_norm(total_of(refs[:-2]), raw_image_ref[...])


def shaped(shape, dtype):
    return jax.ShapeDtypeStruct(shape, dtype)


def call(kernel, outs, ins, specs, out_spec, scratch=(), grant=16, flops=1 << 20):
    return pl.pallas_call(
        kernel,
        out_shape=outs,
        in_specs=specs,
        out_specs=jax.tree.map(lambda _: out_spec, outs),
        scratch_shapes=list(scratch),
        compiler_params=pltpu.CompilerParams(vmem_limit_bytes=grant << 20),
        cost_estimate=pl.CostEstimate(flops=flops, bytes_accessed=1 << 20, transcendentals=0),
    )(*ins)


def bits(count):
    return [1 << i for i in reversed(range((count - 1).bit_length()))]


def make_body(squares, depth):
    plane = 2 * squares
    vmem = pl.BlockSpec(memory_space=pltpu.VMEM)
    smem = pl.BlockSpec(memory_space=pltpu.SMEM)

    def to_line(value, step):
        return lax.ppermute(value, LINE, [(z, z ^ step) for z in range(depth)])

    def to_square(value, step):
        return lax.ppermute(value, SQUARE, [(q, q ^ step) for q in range(squares)])

    def gather_line(value):
        first = bits(depth)[::-1]
        held = lax.optimization_barrier([value] + [to_line(value, s) for s in first])
        blocks = dict(zip([0] + first, held))
        for s in sorted(set(range(depth)) - set(blocks), key=lambda s: bin(s).count("1")):
            near = s & -s
            blocks[s] = to_line(blocks[s ^ near], near)
        return [blocks[s] for s in range(depth)]

    def to_sibling(value):
        return lax.ppermute(value, "core", [(0, 1), (1, 0)])

    def body(student_image, student_text, teacher_image, teacher_text, teacher_scale, student_scale):
        own, width = student_image.shape
        both = width + teacher_image.shape[1]
        images, texts = plane * own, depth * own
        square = lax.axis_index("y") * lax.axis_size("x") + lax.axis_index("x")
        square = square.astype(jnp.int32).reshape(1)
        z = lax.axis_index("z").astype(jnp.int32).reshape(1)
        teacher_scale = teacher_scale.reshape(1)
        student_scale = student_scale.reshape(1)
        grant = 16 if images * texts <= 512 * 256 else 56

        raw_text = side_by_side(student_text, teacher_text)
        raw_texts = gather_line(raw_text)
        raw_image = side_by_side(student_image, teacher_image)
        blocks = [raw_image] + [to_square(raw_image, s) for s in range(1, squares)]

        pupil_text, master_text = call(
            text_unit_kernel,
            (shaped((texts, width), BF16), shaped((texts, both - width), BF16)),
            (z, *raw_texts),
            [smem] + [vmem] * depth,
            vmem,
            grant=grant,
            flops=MANY,
        )
        half = squares * own
        pupil, master = call(
            image_unit_kernel,
            (shaped((half, width), BF16), shaped((half, both - width), BF16)),
            (square, *blocks),
            [smem] + [vmem] * squares,
            vmem,
            grant=grant,
            flops=MANY,
        )
        pupils, masters = (pupil, to_sibling(pupil)), (master, to_sibling(master))
        teach, row_lse, col_lse = call(
            logits_kernel,
            (shaped((images, texts), F32), shaped((2, images), F32), shaped((2, texts), F32)),
            (teacher_scale, student_scale, pupil_text, master_text, *pupils, *masters),
            [smem, smem] + [vmem] * 6,
            vmem,
            grant=grant,
        )

        def joined(parts, flops):
            out = shaped(parts[0].shape, F32)
            return call(join_kernel, out, parts, [vmem] * len(parts), vmem, flops=flops)

        row_lse = call(
            join_sibling_kernel,
            shaped(row_lse.shape, F32),
            (row_lse, to_sibling(row_lse)),
            [vmem] * 2,
            vmem,
        )
        row_lses = [to_square(row_lse, s) for s in range(1, squares)]
        row_lse = joined([row_lse, *row_lses], MANY)
        for s in bits(depth):
            col_lse = joined([col_lse, to_line(col_lse, s)], FEW if s == 1 else SOME)
        block = shaped((own, width), F32)
        sent = shaped((own, width), BF16)
        kept, for_sibling, own_text, *for_line = call(
            weight_kernel,
            (shaped((squares, own, width), F32), shaped((squares, own, width), BF16), block)
            + (sent,) * (depth - 1),
            (z, student_scale, teach, *pupils, pupil_text, col_lse, row_lse),
            [smem] * 2 + [vmem] * 6,
            vmem,
            (pltpu.VMEM((texts, width), F32),),
            grant,
        )
        text_parts = [to_line(part, s + 1) for s, part in enumerate(for_line)]
        text_grad = call(sum_kernel, block, (own_text, *text_parts), [vmem] * depth, vmem, flops=MANY)
        own_image, *for_square = call(
            pair_kernel,
            (block,) + (sent,) * (squares - 1),
            (square, kept, to_sibling(for_sibling)),
            [smem] + [vmem] * 2,
            vmem,
        )
        image_parts = [to_square(part, s + 1) for s, part in reversed(list(enumerate(for_square)))]
        return call(
            back_kernel,
            (block, block),
            (student_image, student_text, text_grad, own_image, *image_parts),
            [vmem] * (3 + squares),
            vmem,
        )

    return body


def solution(mesh):
    named = physical_mesh(mesh)
    split = P(EVERY, None)
    return jax.shard_map(
        make_body(named.shape["y"] * named.shape["x"], named.shape["z"]),
        mesh=named,
        in_specs=(split, split, split, split, P(), P()),
        out_specs=(split, split),
        check_vma=False,
    )
```

```python
import functools

import jax
import jax.numpy as jnp
from jax import lax
from jax.experimental import pallas as pl
from jax.experimental.pallas import tpu as pltpu
from jax.sharding import Mesh, PartitionSpec as P

EPSILON = 1e-12
SQUARE = ("y", "x")
LINE = "z"
EVERY = ("y", "core", "z", "x")
F32 = jnp.float32
BF16 = jnp.bfloat16
FEW, SOME, MANY = 1 << 10, 1 << 31, 1 << 35


def physical_mesh(mesh):
    rows, cols = mesh.shape["row"], mesh.shape["col"]
    side = rows // 2
    wide = side if cols % side == 0 else 1
    return Mesh(mesh.devices.reshape(side, 2, cols // wide, wide), EVERY)


def unit_rows(raw):
    values = raw.astype(F32)
    inverse = lax.rsqrt(jnp.sum(values * values, axis=-1, keepdims=True) + EPSILON)
    return (values * inverse, inverse)


def side_by_side(left, right):
    lowest = jnp.array(-jnp.inf, left.dtype)
    left_width, right_width = left.shape[1], right.shape[1]
    return jnp.maximum(
        lax.pad(left, lowest, ((0, 0, 0), (0, right_width, 0))),
        lax.pad(right, lowest, ((0, 0, 0), (left_width, 0, 0))),
    )


def put_units(block, pupil_ref, master_ref, at):
    at = pl.multiple_of(at, block.shape[0])
    own, width = block.shape[0], pupil_ref.shape[1]
    pupil_ref[pl.ds(at, own), :] = unit_rows(block[:, :width])[0].astype(BF16)
    master_ref[pl.ds(at, own), :] = unit_rows(block[:, width:])[0].astype(BF16)


def image_unit_kernel(square_ref, *refs):
    pupil_ref, master_ref = refs[-2:]
    own = refs[0].shape[0]
    for s, ref in enumerate(refs[:-2]):
        row = pl.multiple_of(jnp.bitwise_xor(square_ref[0], s) * own, own)
        put_units(ref[...], pupil_ref, master_ref, row)


def unit_kernel(raw_ref, out_ref):
    out_ref[...] = unit_rows(raw_ref[...])[0].astype(BF16)


def text_unit_kernel(distances, z_ref, student_ref, teacher_ref, near_ref, *refs):
    pupil_ref, master_ref = refs[-2:]
    own = near_ref.shape[0]

    def place(s):
        return pl.ds(pl.multiple_of(jnp.bitwise_xor(z_ref[0], s) * own, own), own)

    put_units(near_ref[...], pupil_ref, master_ref, jnp.bitwise_xor(z_ref[0], 1) * own)
    unit_kernel(student_ref, pupil_ref.at[place(0)])
    unit_kernel(teacher_ref, master_ref.at[place(0)])
    for k, s in enumerate(distances):
        pupil_ref[place(s), :] = refs[2 * k][...]
        master_ref[place(s), :] = refs[2 * k + 1][...]


def product(left, right):
    return lax.dot_general(left, right, (((1,), (1,)), ((), ())), preferred_element_type=F32)


def block_lse(logits):
    peak = jnp.max(logits, axis=0, keepdims=True)
    return peak + jnp.log(jnp.sum(jnp.exp(logits - peak), axis=0, keepdims=True))


def join_lse(parts):
    top = functools.reduce(jnp.maximum, parts)
    return top + jnp.log(sum(jnp.exp(p - top) for p in parts))


def chunks(pairs):
    half = pairs[0][0].shape[0]
    step = min(512, half)
    return [
        (k * half + at, [pair[k] for pair in pairs], slice(at, at + step))
        for k in range(2)
        for at in range(0, half, step)
    ]


def logits_kernel(
    teacher_scale_ref, student_scale_ref, pupil_text_ref, master_text_ref, pupil_same_ref,
    pupil_other_ref, master_same_ref, master_other_ref, teach_ref, rows_ref, cols_ref,
):
    for k, (scale_ref, pair, text_ref) in enumerate(
        (
            (teacher_scale_ref, (master_same_ref, master_other_ref), master_text_ref),
            (student_scale_ref, (pupil_same_ref, pupil_other_ref), pupil_text_ref),
        )
    ):
        scale = scale_ref[0]
        text = text_ref[...]
        columns = []
        for at, (ref,), part in chunks([pair]):
            image = ref[part, :]
            rows = slice(at, at + image.shape[0])
            logits = scale * product(image, text)
            if k == 0:
                teach_ref[rows, :] = logits
            columns.append(block_lse(logits))
            rows_ref[k : k + 1, rows] = block_lse(scale * product(text, image))
        cols_ref[k : k + 1, :] = join_lse(columns)


def join_kernel(*refs):
    refs[-1][...] = join_lse([ref[...] for ref in refs[:-1]])


def join_sibling_kernel(own_ref, other_ref, out_ref):
    half = own_ref.shape[1] // 2
    for here, there in ((slice(0, half), slice(half, None)), (slice(half, None), slice(0, half))):
        out_ref[:, here] = join_lse([own_ref[:, here], other_ref[:, there]])


def weight_kernel(z_ref, scale_ref, teach_ref, same_ref, other_ref, text_ref, col_ref, row_ref, *refs):
    keep_ref, send_ref, own_text_ref = refs[:3]
    text_out_refs = refs[3:-1]
    text_part_ref = refs[-1]
    squares, own, width = keep_ref.shape
    scale = scale_ref[0]
    col = col_ref[...]
    rows = jnp.concatenate([row_ref[...]] * 4, axis=0)
    text = text_ref[...]
    pairs = [(same_ref, other_ref), (keep_ref, send_ref)]
    pairs[1] = tuple(ref.reshape(squares * own, width) for ref in pairs[1])
    text_part = None
    for at, (image_ref, out_ref), part in chunks(pairs):
        image = image_ref[part, :]
        here = slice(at, at + image.shape[0])
        row = jnp.transpose(rows[:, here])
        teach = teach_ref[here, :]
        learn = scale * product(image, text)
        rows_part = jnp.exp(learn - row[:, 1:2]) - jnp.exp(teach - row[:, 0:1])
        cols_part = jnp.exp(learn - col[1:2, :]) - jnp.exp(teach - col[0:1, :])
        weight = (0.5 * (rows_part + cols_part)).astype(BF16)
        image_part = scale * jnp.dot(weight, text, preferred_element_type=F32)
        out_ref[part, :] = image_part.astype(out_ref.dtype)
        piece = scale * lax.dot_general(
            weight, image, (((0,), (0,)), ((), ())), preferred_element_type=F32
        )
        text_part = piece if text_part is None else text_part + piece
    text_part_ref[...] = text_part
    z = z_ref[0]
    own_text_ref[...] = text_part_ref[pl.ds(pl.multiple_of(z * own, own), own), :]
    for s, ref in enumerate(text_out_refs):
        row = pl.multiple_of(jnp.bitwise_xor(z, s + 1) * own, own)
        ref[...] = text_part_ref[pl.ds(row, own), :].astype(BF16)


def back_norm(grad, raw):
    unit, inverse = unit_rows(raw)
    return inverse * (grad - unit * jnp.sum(unit * grad, axis=-1, keepdims=True))


def pair_kernel(square_ref, kept_ref, received_ref, *refs):
    for s, ref in enumerate(refs):
        at = jnp.bitwise_xor(square_ref[0], s)
        ref[...] = (kept_ref[at] + received_ref[at].astype(F32)).astype(ref.dtype)


def total_of(refs):
    total = refs[0][...]
    for ref in refs[1:]:
        total = total + ref[...].astype(F32)
    return total


def sum_kernel(*refs):
    refs[-1][...] = total_of(refs[:-1])


def back_kernel(raw_image_ref, raw_text_ref, text_ref, *refs):
    image_out_ref, text_out_ref = refs[-2:]
    text_out_ref[...] = back_norm(text_ref[...], raw_text_ref[...])
    image_out_ref[...] = back_norm(total_of(refs[:-2]), raw_image_ref[...])


def shaped(shape, dtype):
    return jax.ShapeDtypeStruct(shape, dtype)


def call(kernel, outs, ins, specs, out_spec, scratch=(), grant=16, flops=1 << 20):
    return pl.pallas_call(
        kernel,
        out_shape=outs,
        in_specs=specs,
        out_specs=jax.tree.map(lambda _: out_spec, outs),
        scratch_shapes=list(scratch),
        compiler_params=pltpu.CompilerParams(vmem_limit_bytes=grant << 20),
        cost_estimate=pl.CostEstimate(flops=flops, bytes_accessed=1 << 20, transcendentals=0),
    )(*ins)


def bits(count):
    return [1 << i for i in reversed(range((count - 1).bit_length()))]


def make_body(squares, depth):
    plane = 2 * squares
    vmem = pl.BlockSpec(memory_space=pltpu.VMEM)
    smem = pl.BlockSpec(memory_space=pltpu.SMEM)

    def to_line(value, step):
        return lax.ppermute(value, LINE, [(z, z ^ step) for z in range(depth)])

    def to_square(value, step):
        return lax.ppermute(value, SQUARE, [(q, q ^ step) for q in range(squares)])

    def gather_square(value):
        first = bits(squares)
        blocks = dict(zip([0] + first, [value] + [to_square(value, s) for s in first]))
        for s in sorted(set(range(squares)) - set(blocks), key=lambda s: bin(s).count("1")):
            hop = s & -s
            blocks[s] = to_square(blocks[s ^ hop], hop)
        return [blocks[s] for s in range(squares)]

    def gather_line(student, teacher):
        far = bits(depth)[:-1]
        parts = [student, teacher]
        units = {s: [to_line(part, s) for part in parts] for s in far}
        near = to_line(side_by_side(student, teacher), 1)
        for s in far:
            units[s][0], near = lax.optimization_barrier((units[s][0], near))
            for k, raw in enumerate(units[s]):
                units[s][k] = call(
                    unit_kernel, shaped(raw.shape, BF16), (raw,), [vmem], vmem, flops=SOME
                )
        rest = set(range(2, depth)) - set(far)
        for s in sorted(rest, key=lambda s: bin(s).count("1")):
            hop = s & -s
            units[s] = [to_line(part, hop) for part in units[s ^ hop]]
        return near, units

    def to_sibling(value):
        return lax.ppermute(value, "core", [(0, 1), (1, 0)])

    def body(student_image, student_text, teacher_image, teacher_text, teacher_scale, student_scale):
        own, width = student_image.shape
        both = width + teacher_image.shape[1]
        images, texts = plane * own, depth * own
        square = lax.axis_index("y") * lax.axis_size("x") + lax.axis_index("x")
        square = square.astype(jnp.int32).reshape(1)
        z = lax.axis_index("z").astype(jnp.int32).reshape(1)
        teacher_scale = teacher_scale.reshape(1)
        student_scale = student_scale.reshape(1)
        grant = 16 if images * texts <= 512 * 256 else 56

        raw_image = side_by_side(student_image, teacher_image)
        blocks = gather_square(raw_image)
        near, units = gather_line(student_text, teacher_text)
        raw_texts = [student_text, teacher_text, near] + sum(units.values(), [])

        pupil_text, master_text = call(
            functools.partial(text_unit_kernel, tuple(units)),
            (shaped((texts, width), BF16), shaped((texts, both - width), BF16)),
            (z, *raw_texts),
            [smem] + [vmem] * len(raw_texts),
            vmem,
            grant=grant,
            flops=MANY,
        )
        half = squares * own
        pupil, master = call(
            image_unit_kernel,
            (shaped((half, width), BF16), shaped((half, both - width), BF16)),
            (square, *blocks),
            [smem] + [vmem] * squares,
            vmem,
            grant=grant,
            flops=MANY,
        )
        pupils, masters = (pupil, to_sibling(pupil)), (master, to_sibling(master))
        teach, row_lse, col_lse = call(
            logits_kernel,
            (shaped((images, texts), F32), shaped((2, images), F32), shaped((2, texts), F32)),
            (teacher_scale, student_scale, pupil_text, master_text, *pupils, *masters),
            [smem, smem] + [vmem] * 6,
            vmem,
            grant=grant,
        )

        def joined(parts, flops):
            out = shaped(parts[0].shape, F32)
            return call(join_kernel, out, parts, [vmem] * len(parts), vmem, flops=flops)

        row_lse = call(
            join_sibling_kernel,
            shaped(row_lse.shape, F32),
            (row_lse, to_sibling(row_lse)),
            [vmem] * 2,
            vmem,
        )
        row_lses = [to_square(row_lse, s) for s in range(1, squares)]
        row_lse = joined([row_lse, *row_lses], MANY)
        for s in bits(depth):
            col_lse = joined([col_lse, to_line(col_lse, s)], FEW if s == 1 else SOME)
        block = shaped((own, width), F32)
        sent = shaped((own, width), BF16)
        kept, for_sibling, own_text, *for_line = call(
            weight_kernel,
            (shaped((squares, own, width), F32), shaped((squares, own, width), BF16), block)
            + (sent,) * (depth - 1),
            (z, student_scale, teach, *pupils, pupil_text, col_lse, row_lse),
            [smem] * 2 + [vmem] * 6,
            vmem,
            (pltpu.VMEM((texts, width), F32),),
            grant,
        )
        text_parts = [to_line(part, s + 1) for s, part in enumerate(for_line)]
        text_grad = call(sum_kernel, block, (own_text, *text_parts), [vmem] * depth, vmem, flops=MANY)
        own_image, *for_square = call(
            pair_kernel,
            (block,) + (sent,) * (squares - 1),
            (square, kept, to_sibling(for_sibling)),
            [smem] + [vmem] * 2,
            vmem,
        )
        image_parts = [to_square(part, s + 1) for s, part in reversed(list(enumerate(for_square)))]
        return call(
            back_kernel,
            (block, block),
            (student_image, student_text, text_grad, own_image, *image_parts),
            [vmem] * (3 + squares),
            vmem,
        )

    return body


def solution(mesh):
    named = physical_mesh(mesh)
    split = P(EVERY, None)
    return jax.shard_map(
        make_body(named.shape["y"] * named.shape["x"], named.shape["z"]),
        mesh=named,
        in_specs=(split, split, split, split, P(), P()),
        out_specs=(split, split),
        check_vma=False,
    )
```

```python
import functools

import jax
import jax.numpy as jnp
from jax import lax
from jax.experimental import pallas as pl
from jax.experimental.pallas import tpu as pltpu
from jax.sharding import Mesh, PartitionSpec as P

EPSILON = 1e-12
SQUARE = ("y", "x")
LINE = "z"
EVERY = ("y", "core", "z", "x")
F32 = jnp.float32
BF16 = jnp.bfloat16
FEW, SOME, MANY = 1 << 10, 1 << 31, 1 << 35


def physical_mesh(mesh):
    rows, cols = mesh.shape["row"], mesh.shape["col"]
    side = rows // 2
    wide = side if cols % side == 0 else 1
    return Mesh(mesh.devices.reshape(side, 2, cols // wide, wide), EVERY)


def unit_rows(raw):
    values = raw.astype(F32)
    inverse = lax.rsqrt(jnp.sum(values * values, axis=-1, keepdims=True) + EPSILON)
    return (values * inverse, inverse)


def side_by_side(left, right):
    lowest = jnp.array(-jnp.inf, left.dtype)
    left_width, right_width = left.shape[1], right.shape[1]
    return jnp.maximum(
        lax.pad(left, lowest, ((0, 0, 0), (0, right_width, 0))),
        lax.pad(right, lowest, ((0, 0, 0), (left_width, 0, 0))),
    )


def put_units(block, pupil_ref, master_ref, at):
    at = pl.multiple_of(at, block.shape[0])
    own, width = block.shape[0], pupil_ref.shape[1]
    pupil_ref[pl.ds(at, own), :] = unit_rows(block[:, :width])[0].astype(BF16)
    master_ref[pl.ds(at, own), :] = unit_rows(block[:, width:])[0].astype(BF16)


def image_unit_kernel(square_ref, *refs):
    pupil_ref, master_ref = refs[-2:]
    own = refs[0].shape[0]
    for s, ref in enumerate(refs[:-2]):
        row = pl.multiple_of(jnp.bitwise_xor(square_ref[0], s) * own, own)
        put_units(ref[...], pupil_ref, master_ref, row)


def unit_kernel(raw_ref, out_ref):
    out_ref[...] = unit_rows(raw_ref[...])[0].astype(BF16)


def text_unit_kernel(distances, z_ref, student_ref, teacher_ref, near_ref, *refs):
    pupil_ref, master_ref = refs[-2:]
    own = near_ref.shape[0]

    def place(s):
        return pl.ds(pl.multiple_of(jnp.bitwise_xor(z_ref[0], s) * own, own), own)

    put_units(near_ref[...], pupil_ref, master_ref, jnp.bitwise_xor(z_ref[0], 1) * own)
    unit_kernel(student_ref, pupil_ref.at[place(0)])
    unit_kernel(teacher_ref, master_ref.at[place(0)])
    for k, s in enumerate(distances):
        pupil_ref[place(s), :] = refs[2 * k][...]
        master_ref[place(s), :] = refs[2 * k + 1][...]


def product(left, right):
    return lax.dot_general(left, right, (((1,), (1,)), ((), ())), preferred_element_type=F32)


def block_lse(logits):
    peak = jnp.max(logits, axis=0, keepdims=True)
    return peak + jnp.log(jnp.sum(jnp.exp(logits - peak), axis=0, keepdims=True))


def join_lse(parts):
    top = functools.reduce(jnp.maximum, parts)
    return top + jnp.log(sum(jnp.exp(p - top) for p in parts))


def chunks(pairs):
    half = pairs[0][0].shape[0]
    step = min(512, half)
    return [
        (k * half + at, [pair[k] for pair in pairs], slice(at, at + step))
        for k in range(2)
        for at in range(0, half, step)
    ]


def logits_kernel(
    teacher_scale_ref, student_scale_ref, pupil_text_ref, master_text_ref, pupil_same_ref,
    pupil_other_ref, master_same_ref, master_other_ref, teach_ref, rows_ref, cols_ref,
):
    for k, (scale_ref, pair, text_ref) in enumerate(
        (
            (teacher_scale_ref, (master_same_ref, master_other_ref), master_text_ref),
            (student_scale_ref, (pupil_same_ref, pupil_other_ref), pupil_text_ref),
        )
    ):
        scale = scale_ref[0]
        text = text_ref[...]
        columns = []
        for at, (ref,), part in chunks([pair]):
            image = ref[part, :]
            rows = slice(at, at + image.shape[0])
            logits = scale * product(image, text)
            if k == 0:
                teach_ref[rows, :] = logits
            columns.append(block_lse(logits))
            rows_ref[k : k + 1, rows] = block_lse(scale * product(text, image))
        cols_ref[k : k + 1, :] = join_lse(columns)


def join_kernel(*refs):
    refs[-1][...] = join_lse([ref[...] for ref in refs[:-1]])


def join_sibling_kernel(own_ref, other_ref, out_ref):
    half = own_ref.shape[1] // 2
    for here, there in ((slice(0, half), slice(half, None)), (slice(half, None), slice(0, half))):
        out_ref[:, here] = join_lse([own_ref[:, here], other_ref[:, there]])


def weight_kernel(z_ref, scale_ref, teach_ref, same_ref, other_ref, text_ref, col_ref, row_ref, *refs):
    keep_ref, send_ref, own_text_ref = refs[:3]
    text_out_refs = refs[3:-1]
    text_part_ref = refs[-1]
    squares, own, width = keep_ref.shape
    scale = scale_ref[0]
    col = col_ref[...]
    rows = jnp.concatenate([row_ref[...]] * 4, axis=0)
    text = text_ref[...]
    pairs = [(same_ref, other_ref), (keep_ref, send_ref)]
    pairs[1] = tuple(ref.reshape(squares * own, width) for ref in pairs[1])
    text_part = None
    for at, (image_ref, out_ref), part in chunks(pairs):
        image = image_ref[part, :]
        here = slice(at, at + image.shape[0])
        row = jnp.transpose(rows[:, here])
        teach = teach_ref[here, :]
        learn = scale * product(image, text)
        rows_part = jnp.exp(learn - row[:, 1:2]) - jnp.exp(teach - row[:, 0:1])
        cols_part = jnp.exp(learn - col[1:2, :]) - jnp.exp(teach - col[0:1, :])
        weight = (0.5 * (rows_part + cols_part)).astype(BF16)
        image_part = scale * jnp.dot(weight, text, preferred_element_type=F32)
        out_ref[part, :] = image_part.astype(out_ref.dtype)
        piece = scale * lax.dot_general(
            weight, image, (((0,), (0,)), ((), ())), preferred_element_type=F32
        )
        text_part = piece if text_part is None else text_part + piece
    text_part_ref[...] = text_part
    z = z_ref[0]
    own_text_ref[...] = text_part_ref[pl.ds(pl.multiple_of(z * own, own), own), :]
    for s, ref in enumerate(text_out_refs):
        row = pl.multiple_of(jnp.bitwise_xor(z, s + 1) * own, own)
        ref[...] = text_part_ref[pl.ds(row, own), :].astype(BF16)


def back_norm(grad, raw):
    unit, inverse = unit_rows(raw)
    return inverse * (grad - unit * jnp.sum(unit * grad, axis=-1, keepdims=True))


def pair_kernel(square_ref, kept_ref, received_ref, *refs):
    for s, ref in enumerate(refs):
        at = jnp.bitwise_xor(square_ref[0], s)
        ref[...] = (kept_ref[at] + received_ref[at].astype(F32)).astype(ref.dtype)


def total_of(refs):
    total = refs[0][...]
    for ref in refs[1:]:
        total = total + ref[...].astype(F32)
    return total


def sum_kernel(*refs):
    refs[-1][...] = total_of(refs[:-1])


def back_kernel(raw_image_ref, raw_text_ref, text_ref, *refs):
    image_out_ref, text_out_ref = refs[-2:]
    text_out_ref[...] = back_norm(text_ref[...], raw_text_ref[...])
    image_out_ref[...] = back_norm(total_of(refs[:-2]), raw_image_ref[...])


def shaped(shape, dtype):
    return jax.ShapeDtypeStruct(shape, dtype)


def call(kernel, outs, ins, specs, out_spec, scratch=(), grant=16, flops=1 << 20):
    return pl.pallas_call(
        kernel,
        out_shape=outs,
        in_specs=specs,
        out_specs=jax.tree.map(lambda _: out_spec, outs),
        scratch_shapes=list(scratch),
        compiler_params=pltpu.CompilerParams(vmem_limit_bytes=grant << 20),
        cost_estimate=pl.CostEstimate(flops=flops, bytes_accessed=1 << 20, transcendentals=0),
    )(*ins)


def bits(count):
    return [1 << i for i in reversed(range((count - 1).bit_length()))]


def make_body(squares, depth):
    plane = 2 * squares
    vmem = pl.BlockSpec(memory_space=pltpu.VMEM)
    smem = pl.BlockSpec(memory_space=pltpu.SMEM)

    def to_line(value, step):
        return lax.ppermute(value, LINE, [(z, z ^ step) for z in range(depth)])

    def to_square(value, step):
        return lax.ppermute(value, SQUARE, [(q, q ^ step) for q in range(squares)])

    def gather_square(value):
        first = bits(squares)
        held = lax.optimization_barrier([value] + [to_square(value, s) for s in first])
        blocks = dict(zip([0] + first, held))
        for s in sorted(set(range(squares)) - set(blocks), key=lambda s: bin(s).count("1")):
            hop = s & -s
            blocks[s] = to_square(blocks[s ^ hop], hop)
        return [blocks[s] for s in range(squares)]

    def gather_line(student, teacher):
        far = bits(depth)[:-1]
        parts = [student, teacher]
        units = {s: [to_line(part, s) for part in parts] for s in far}
        near = to_line(side_by_side(student, teacher), 1)
        for s in far:
            units[s][0], near = lax.optimization_barrier((units[s][0], near))
            for k, raw in enumerate(units[s]):
                units[s][k] = call(
                    unit_kernel, shaped(raw.shape, BF16), (raw,), [vmem], vmem, flops=SOME
                )
        rest = set(range(2, depth)) - set(far)
        for s in sorted(rest, key=lambda s: bin(s).count("1")):
            hop = s & -s
            units[s] = [to_line(part, hop) for part in units[s ^ hop]]
        return near, units

    def to_sibling(value):
        return lax.ppermute(value, "core", [(0, 1), (1, 0)])

    def body(student_image, student_text, teacher_image, teacher_text, teacher_scale, student_scale):
        own, width = student_image.shape
        both = width + teacher_image.shape[1]
        images, texts = plane * own, depth * own
        square = lax.axis_index("y") * lax.axis_size("x") + lax.axis_index("x")
        square = square.astype(jnp.int32).reshape(1)
        z = lax.axis_index("z").astype(jnp.int32).reshape(1)
        teacher_scale = teacher_scale.reshape(1)
        student_scale = student_scale.reshape(1)
        grant = 16 if images * texts <= 512 * 256 else 56

        raw_image = side_by_side(student_image, teacher_image)
        blocks = gather_square(raw_image)
        near, units = gather_line(student_text, teacher_text)
        raw_texts = [student_text, teacher_text, near] + sum(units.values(), [])

        pupil_text, master_text = call(
            functools.partial(text_unit_kernel, tuple(units)),
            (shaped((texts, width), BF16), shaped((texts, both - width), BF16)),
            (z, *raw_texts),
            [smem] + [vmem] * len(raw_texts),
            vmem,
            grant=grant,
            flops=MANY,
        )
        half = squares * own
        pupil, master = call(
            image_unit_kernel,
            (shaped((half, width), BF16), shaped((half, both - width), BF16)),
            (square, *blocks),
            [smem] + [vmem] * squares,
            vmem,
            grant=grant,
            flops=MANY,
        )
        pupils, masters = (pupil, to_sibling(pupil)), (master, to_sibling(master))
        teach, row_lse, col_lse = call(
            logits_kernel,
            (shaped((images, texts), F32), shaped((2, images), F32), shaped((2, texts), F32)),
            (teacher_scale, student_scale, pupil_text, master_text, *pupils, *masters),
            [smem, smem] + [vmem] * 6,
            vmem,
            grant=grant,
        )

        def joined(parts, flops):
            out = shaped(parts[0].shape, F32)
            return call(join_kernel, out, parts, [vmem] * len(parts), vmem, flops=flops)

        row_lse = call(
            join_sibling_kernel,
            shaped(row_lse.shape, F32),
            (row_lse, to_sibling(row_lse)),
            [vmem] * 2,
            vmem,
        )
        row_lses = [to_square(row_lse, s) for s in range(1, squares)]
        row_lse = joined([row_lse, *row_lses], MANY)
        for s in bits(depth):
            col_lse = joined([col_lse, to_line(col_lse, s)], FEW if s == 1 else SOME)
        block = shaped((own, width), F32)
        sent = shaped((own, width), BF16)
        kept, for_sibling, own_text, *for_line = call(
            weight_kernel,
            (shaped((squares, own, width), F32), shaped((squares, own, width), BF16), block)
            + (sent,) * (depth - 1),
            (z, student_scale, teach, *pupils, pupil_text, col_lse, row_lse),
            [smem] * 2 + [vmem] * 6,
            vmem,
            (pltpu.VMEM((texts, width), F32),),
            grant,
        )
        text_parts = [to_line(part, s + 1) for s, part in enumerate(for_line)]
        text_grad = call(sum_kernel, block, (own_text, *text_parts), [vmem] * depth, vmem, flops=MANY)
        own_image, *for_square = call(
            pair_kernel,
            (block,) + (sent,) * (squares - 1),
            (square, kept, to_sibling(for_sibling)),
            [smem] + [vmem] * 2,
            vmem,
        )
        image_parts = [to_square(part, s + 1) for s, part in reversed(list(enumerate(for_square)))]
        return call(
            back_kernel,
            (block, block),
            (student_image, student_text, text_grad, own_image, *image_parts),
            [vmem] * (3 + squares),
            vmem,
        )

    return body


def solution(mesh):
    named = physical_mesh(mesh)
    split = P(EVERY, None)
    return jax.shard_map(
        make_body(named.shape["y"] * named.shape["x"], named.shape["z"]),
        mesh=named,
        in_specs=(split, split, split, split, P(), P()),
        out_specs=(split, split),
        check_vma=False,
    )
```

```python
import functools

import jax
import jax.numpy as jnp
from jax import lax
from jax.experimental import pallas as pl
from jax.experimental.pallas import tpu as pltpu
from jax.sharding import Mesh, PartitionSpec as P

EPSILON = 1e-12
SQUARE = ("y", "x")
LINE = "z"
EVERY = ("y", "core", "z", "x")
F32 = jnp.float32
BF16 = jnp.bfloat16
FEW, SOME, MANY = 1 << 10, 1 << 31, 1 << 35


def physical_mesh(mesh):
    rows, cols = mesh.shape["row"], mesh.shape["col"]
    side = rows // 2
    wide = side if cols % side == 0 else 1
    return Mesh(mesh.devices.reshape(side, 2, cols // wide, wide), EVERY)


def unit_rows(raw):
    values = raw.astype(F32)
    inverse = lax.rsqrt(jnp.sum(values * values, axis=-1, keepdims=True) + EPSILON)
    return (values * inverse, inverse)


def side_by_side(left, right):
    lowest = jnp.array(-jnp.inf, left.dtype)
    left_width, right_width = left.shape[1], right.shape[1]
    return jnp.maximum(
        lax.pad(left, lowest, ((0, 0, 0), (0, right_width, 0))),
        lax.pad(right, lowest, ((0, 0, 0), (left_width, 0, 0))),
    )


def put_units(block, pupil_ref, master_ref, at):
    at = pl.multiple_of(at, block.shape[0])
    own, width = block.shape[0], pupil_ref.shape[1]
    pupil_ref[pl.ds(at, own), :] = unit_rows(block[:, :width])[0].astype(BF16)
    master_ref[pl.ds(at, own), :] = unit_rows(block[:, width:])[0].astype(BF16)


def image_unit_kernel(square_ref, *refs):
    pupil_ref, master_ref = refs[-2:]
    own = refs[0].shape[0]
    for s, ref in enumerate(refs[:-2]):
        row = pl.multiple_of(jnp.bitwise_xor(square_ref[0], s) * own, own)
        put_units(ref[...], pupil_ref, master_ref, row)


def unit_kernel(raw_ref, out_ref):
    out_ref[...] = unit_rows(raw_ref[...])[0].astype(BF16)


def text_unit_kernel(distances, z_ref, student_ref, teacher_ref, near_ref, *refs):
    pupil_ref, master_ref = refs[-2:]
    own = near_ref.shape[0]

    def place(s):
        return pl.ds(pl.multiple_of(jnp.bitwise_xor(z_ref[0], s) * own, own), own)

    put_units(near_ref[...], pupil_ref, master_ref, jnp.bitwise_xor(z_ref[0], 1) * own)
    unit_kernel(student_ref, pupil_ref.at[place(0)])
    unit_kernel(teacher_ref, master_ref.at[place(0)])
    for k, s in enumerate(distances):
        pupil_ref[place(s), :] = refs[2 * k][...]
        master_ref[place(s), :] = refs[2 * k + 1][...]


def product(left, right):
    return lax.dot_general(left, right, (((1,), (1,)), ((), ())), preferred_element_type=F32)


def block_lse(logits):
    peak = jnp.max(logits, axis=0, keepdims=True)
    return peak + jnp.log(jnp.sum(jnp.exp(logits - peak), axis=0, keepdims=True))


def join_lse(parts):
    top = functools.reduce(jnp.maximum, parts)
    return top + jnp.log(sum(jnp.exp(p - top) for p in parts))


def chunks(pairs):
    half = pairs[0][0].shape[0]
    step = min(512, half)
    return [
        (k * half + at, [pair[k] for pair in pairs], slice(at, at + step))
        for k in range(2)
        for at in range(0, half, step)
    ]


def logits_kernel(
    teacher_scale_ref, student_scale_ref, pupil_text_ref, master_text_ref, pupil_same_ref,
    pupil_other_ref, master_same_ref, master_other_ref, teach_ref, rows_ref, cols_ref,
):
    for k, (scale_ref, pair, text_ref) in enumerate(
        (
            (teacher_scale_ref, (master_same_ref, master_other_ref), master_text_ref),
            (student_scale_ref, (pupil_same_ref, pupil_other_ref), pupil_text_ref),
        )
    ):
        scale = scale_ref[0]
        text = text_ref[...]
        columns = []
        for at, (ref,), part in chunks([pair]):
            image = ref[part, :]
            rows = slice(at, at + image.shape[0])
            logits = scale * product(image, text)
            if k == 0:
                teach_ref[rows, :] = logits
            columns.append(block_lse(logits))
            rows_ref[k : k + 1, rows] = block_lse(scale * product(text, image))
        cols_ref[k : k + 1, :] = join_lse(columns)


def join_kernel(*refs):
    refs[-1][...] = join_lse([ref[...] for ref in refs[:-1]])


def join_sibling_kernel(own_ref, other_ref, out_ref):
    half = own_ref.shape[1] // 2
    for here, there in ((slice(0, half), slice(half, None)), (slice(half, None), slice(0, half))):
        out_ref[:, here] = join_lse([own_ref[:, here], other_ref[:, there]])


def weight_kernel(z_ref, scale_ref, teach_ref, same_ref, other_ref, text_ref, col_ref, row_ref, *refs):
    keep_ref, send_ref, own_text_ref = refs[:3]
    text_out_refs = refs[3:-1]
    text_part_ref = refs[-1]
    squares, own, width = keep_ref.shape
    scale = scale_ref[0]
    col = col_ref[...]
    rows = jnp.concatenate([row_ref[...]] * 4, axis=0)
    text = text_ref[...]
    pairs = [(same_ref, other_ref), (keep_ref, send_ref)]
    pairs[1] = tuple(ref.reshape(squares * own, width) for ref in pairs[1])
    text_part = None
    for at, (image_ref, out_ref), part in chunks(pairs):
        image = image_ref[part, :]
        here = slice(at, at + image.shape[0])
        row = jnp.transpose(rows[:, here])
        teach = teach_ref[here, :]
        learn = scale * product(image, text)
        rows_part = jnp.exp(learn - row[:, 1:2]) - jnp.exp(teach - row[:, 0:1])
        cols_part = jnp.exp(learn - col[1:2, :]) - jnp.exp(teach - col[0:1, :])
        weight = (0.5 * (rows_part + cols_part)).astype(BF16)
        image_part = scale * jnp.dot(weight, text, preferred_element_type=F32)
        out_ref[part, :] = image_part.astype(out_ref.dtype)
        piece = scale * lax.dot_general(
            weight, image, (((0,), (0,)), ((), ())), preferred_element_type=F32
        )
        text_part = piece if text_part is None else text_part + piece
    text_part_ref[...] = text_part
    z = z_ref[0]
    own_text_ref[...] = text_part_ref[pl.ds(pl.multiple_of(z * own, own), own), :]
    for s, ref in enumerate(text_out_refs):
        row = pl.multiple_of(jnp.bitwise_xor(z, s + 1) * own, own)
        ref[...] = text_part_ref[pl.ds(row, own), :].astype(BF16)


def back_norm(grad, raw):
    unit, inverse = unit_rows(raw)
    return inverse * (grad - unit * jnp.sum(unit * grad, axis=-1, keepdims=True))


def pair_kernel(square_ref, kept_ref, received_ref, *refs):
    for s, ref in enumerate(refs):
        at = jnp.bitwise_xor(square_ref[0], s)
        ref[...] = (kept_ref[at] + received_ref[at].astype(F32)).astype(ref.dtype)


def total_of(refs):
    total = refs[0][...]
    for ref in refs[1:]:
        total = total + ref[...].astype(F32)
    return total


def sum_kernel(*refs):
    refs[-1][...] = total_of(refs[:-1])


def back_kernel(raw_image_ref, raw_text_ref, text_ref, *refs):
    image_out_ref, text_out_ref = refs[-2:]
    text_out_ref[...] = back_norm(text_ref[...], raw_text_ref[...])
    image_out_ref[...] = back_norm(total_of(refs[:-2]), raw_image_ref[...])


def shaped(shape, dtype):
    return jax.ShapeDtypeStruct(shape, dtype)


def call(kernel, outs, ins, specs, out_spec, scratch=(), grant=16, flops=1 << 20):
    return pl.pallas_call(
        kernel,
        out_shape=outs,
        in_specs=specs,
        out_specs=jax.tree.map(lambda _: out_spec, outs),
        scratch_shapes=list(scratch),
        compiler_params=pltpu.CompilerParams(vmem_limit_bytes=grant << 20),
        cost_estimate=pl.CostEstimate(flops=flops, bytes_accessed=1 << 20, transcendentals=0),
    )(*ins)


def bits(count):
    return [1 << i for i in reversed(range((count - 1).bit_length()))]


def make_body(squares, depth):
    plane = 2 * squares
    vmem = pl.BlockSpec(memory_space=pltpu.VMEM)
    smem = pl.BlockSpec(memory_space=pltpu.SMEM)

    def to_line(value, step):
        return lax.ppermute(value, LINE, [(z, z ^ step) for z in range(depth)])

    def to_square(value, step):
        return lax.ppermute(value, SQUARE, [(q, q ^ step) for q in range(squares)])

    def gather_square(value):
        first = bits(squares)
        blocks = dict(zip([0] + first, [value] + [to_square(value, s) for s in first]))
        for s in sorted(set(range(squares)) - set(blocks), key=lambda s: bin(s).count("1")):
            hop = s & -s
            blocks[s] = to_square(blocks[s ^ hop], hop)
        return [blocks[s] for s in range(squares)]

    def gather_line(student, teacher, plane_block):
        far = bits(depth)[:-1]
        parts = [student, teacher]
        units = {s: [to_line(part, s) for part in parts] for s in far}
        near = to_line(side_by_side(student, teacher), 1)
        for s in far:
            units[s][0], near, plane_block = lax.optimization_barrier((units[s][0], near, plane_block))
            for k, raw in enumerate(units[s]):
                units[s][k] = call(
                    unit_kernel, shaped(raw.shape, BF16), (raw,), [vmem], vmem, flops=SOME
                )
        rest = set(range(2, depth)) - set(far)
        for s in sorted(rest, key=lambda s: bin(s).count("1")):
            hop = s & -s
            units[s] = [to_line(part, hop) for part in units[s ^ hop]]
        return near, units, plane_block

    def to_sibling(value):
        return lax.ppermute(value, "core", [(0, 1), (1, 0)])

    def body(student_image, student_text, teacher_image, teacher_text, teacher_scale, student_scale):
        own, width = student_image.shape
        both = width + teacher_image.shape[1]
        images, texts = plane * own, depth * own
        square = lax.axis_index("y") * lax.axis_size("x") + lax.axis_index("x")
        square = square.astype(jnp.int32).reshape(1)
        z = lax.axis_index("z").astype(jnp.int32).reshape(1)
        teacher_scale = teacher_scale.reshape(1)
        student_scale = student_scale.reshape(1)
        grant = 16 if images * texts <= 512 * 256 else 56

        raw_image = side_by_side(student_image, teacher_image)
        blocks = gather_square(raw_image)
        near, units, blocks[1] = gather_line(student_text, teacher_text, blocks[1])
        raw_texts = [student_text, teacher_text, near] + sum(units.values(), [])

        pupil_text, master_text = call(
            functools.partial(text_unit_kernel, tuple(units)),
            (shaped((texts, width), BF16), shaped((texts, both - width), BF16)),
            (z, *raw_texts),
            [smem] + [vmem] * len(raw_texts),
            vmem,
            grant=grant,
            flops=MANY,
        )
        half = squares * own
        pupil, master = call(
            image_unit_kernel,
            (shaped((half, width), BF16), shaped((half, both - width), BF16)),
            (square, *blocks),
            [smem] + [vmem] * squares,
            vmem,
            grant=grant,
            flops=MANY,
        )
        pupils, masters = (pupil, to_sibling(pupil)), (master, to_sibling(master))
        teach, row_lse, col_lse = call(
            logits_kernel,
            (shaped((images, texts), F32), shaped((2, images), F32), shaped((2, texts), F32)),
            (teacher_scale, student_scale, pupil_text, master_text, *pupils, *masters),
            [smem, smem] + [vmem] * 6,
            vmem,
            grant=grant,
        )

        def joined(parts, flops):
            out = shaped(parts[0].shape, F32)
            return call(join_kernel, out, parts, [vmem] * len(parts), vmem, flops=flops)

        row_lse = call(
            join_sibling_kernel,
            shaped(row_lse.shape, F32),
            (row_lse, to_sibling(row_lse)),
            [vmem] * 2,
            vmem,
        )
        row_lses = [to_square(row_lse, s) for s in range(1, squares)]
        row_lse = joined([row_lse, *row_lses], MANY)
        for s in bits(depth):
            col_lse = joined([col_lse, to_line(col_lse, s)], FEW if s == 1 else SOME)
        block = shaped((own, width), F32)
        sent = shaped((own, width), BF16)
        kept, for_sibling, own_text, *for_line = call(
            weight_kernel,
            (shaped((squares, own, width), F32), shaped((squares, own, width), BF16), block)
            + (sent,) * (depth - 1),
            (z, student_scale, teach, *pupils, pupil_text, col_lse, row_lse),
            [smem] * 2 + [vmem] * 6,
            vmem,
            (pltpu.VMEM((texts, width), F32),),
            grant,
        )
        text_parts = [to_line(part, s + 1) for s, part in enumerate(for_line)]
        text_grad = call(sum_kernel, block, (own_text, *text_parts), [vmem] * depth, vmem, flops=MANY)
        own_image, *for_square = call(
            pair_kernel,
            (block,) + (sent,) * (squares - 1),
            (square, kept, to_sibling(for_sibling)),
            [smem] + [vmem] * 2,
            vmem,
        )
        image_parts = [to_square(part, s + 1) for s, part in reversed(list(enumerate(for_square)))]
        return call(
            back_kernel,
            (block, block),
            (student_image, student_text, text_grad, own_image, *image_parts),
            [vmem] * (3 + squares),
            vmem,
        )

    return body


def solution(mesh):
    named = physical_mesh(mesh)
    split = P(EVERY, None)
    return jax.shard_map(
        make_body(named.shape["y"] * named.shape["x"], named.shape["z"]),
        mesh=named,
        in_specs=(split, split, split, split, P(), P()),
        out_specs=(split, split),
        check_vma=False,
    )
```

```python
import functools

import jax
import jax.numpy as jnp
from jax import lax
from jax.experimental import pallas as pl
from jax.experimental.pallas import tpu as pltpu
from jax.sharding import Mesh, PartitionSpec as P

EPSILON = 1e-12
SQUARE = ("y", "x")
LINE = "z"
EVERY = ("y", "core", "z", "x")
F32 = jnp.float32
BF16 = jnp.bfloat16
FEW, SOME, MANY = 1 << 10, 1 << 31, 1 << 35


def physical_mesh(mesh):
    rows, cols = mesh.shape["row"], mesh.shape["col"]
    side = rows // 2
    wide = side if cols % side == 0 else 1
    return Mesh(mesh.devices.reshape(side, 2, cols // wide, wide), EVERY)


def unit_rows(raw):
    values = raw.astype(F32)
    inverse = lax.rsqrt(jnp.sum(values * values, axis=-1, keepdims=True) + EPSILON)
    return (values * inverse, inverse)


def side_by_side(left, right):
    lowest = jnp.array(-jnp.inf, left.dtype)
    left_width, right_width = left.shape[1], right.shape[1]
    return jnp.maximum(
        lax.pad(left, lowest, ((0, 0, 0), (0, right_width, 0))),
        lax.pad(right, lowest, ((0, 0, 0), (left_width, 0, 0))),
    )


def put_units(block, pupil_ref, master_ref, at):
    at = pl.multiple_of(at, block.shape[0])
    own, width = block.shape[0], pupil_ref.shape[1]
    pupil_ref[pl.ds(at, own), :] = unit_rows(block[:, :width])[0].astype(BF16)
    master_ref[pl.ds(at, own), :] = unit_rows(block[:, width:])[0].astype(BF16)


def image_unit_kernel(square_ref, *refs):
    pupil_ref, master_ref = refs[-2:]
    own = refs[0].shape[0]
    for s, ref in enumerate(refs[:-2]):
        row = pl.multiple_of(jnp.bitwise_xor(square_ref[0], s) * own, own)
        put_units(ref[...], pupil_ref, master_ref, row)


def unit_kernel(raw_ref, out_ref):
    out_ref[...] = unit_rows(raw_ref[...])[0].astype(BF16)


def text_unit_kernel(distances, z_ref, student_ref, teacher_ref, near_ref, *refs):
    pupil_ref, master_ref = refs[-2:]
    own = near_ref.shape[0]

    def place(s):
        return pl.ds(pl.multiple_of(jnp.bitwise_xor(z_ref[0], s) * own, own), own)

    put_units(near_ref[...], pupil_ref, master_ref, jnp.bitwise_xor(z_ref[0], 1) * own)
    unit_kernel(student_ref, pupil_ref.at[place(0)])
    unit_kernel(teacher_ref, master_ref.at[place(0)])
    for k, s in enumerate(distances):
        pupil_ref[place(s), :] = refs[2 * k][...]
        master_ref[place(s), :] = refs[2 * k + 1][...]


def product(left, right):
    return lax.dot_general(left, right, (((1,), (1,)), ((), ())), preferred_element_type=F32)


def block_lse(logits):
    peak = jnp.max(logits, axis=0, keepdims=True)
    return peak + jnp.log(jnp.sum(jnp.exp(logits - peak), axis=0, keepdims=True))


def join_lse(parts):
    top = functools.reduce(jnp.maximum, parts)
    return top + jnp.log(sum(jnp.exp(p - top) for p in parts))


def chunks(pairs):
    half = pairs[0][0].shape[0]
    step = min(512, half)
    return [
        (k * half + at, [pair[k] for pair in pairs], slice(at, at + step))
        for k in range(2)
        for at in range(0, half, step)
    ]


def logits_kernel(
    teacher_scale_ref, student_scale_ref, pupil_text_ref, master_text_ref, pupil_same_ref,
    pupil_other_ref, master_same_ref, master_other_ref, teach_ref, rows_ref, cols_ref,
):
    for k, (scale_ref, pair, text_ref) in enumerate(
        (
            (teacher_scale_ref, (master_same_ref, master_other_ref), master_text_ref),
            (student_scale_ref, (pupil_same_ref, pupil_other_ref), pupil_text_ref),
        )
    ):
        scale = scale_ref[0]
        text = text_ref[...]
        columns = []
        for at, (ref,), part in chunks([pair]):
            image = ref[part, :]
            rows = slice(at, at + image.shape[0])
            logits = scale * product(image, text)
            if k == 0:
                teach_ref[rows, :] = logits
            columns.append(block_lse(logits))
            rows_ref[k : k + 1, rows] = block_lse(scale * product(text, image))
        cols_ref[k : k + 1, :] = join_lse(columns)


def join_kernel(*refs):
    refs[-1][...] = join_lse([ref[...] for ref in refs[:-1]])


def join_sibling_kernel(own_ref, other_ref, out_ref):
    half = own_ref.shape[1] // 2
    for here, there in ((slice(0, half), slice(half, None)), (slice(half, None), slice(0, half))):
        out_ref[:, here] = join_lse([own_ref[:, here], other_ref[:, there]])


def weight_kernel(z_ref, scale_ref, teach_ref, same_ref, other_ref, text_ref, col_ref, row_ref, *refs):
    keep_ref, send_ref, own_text_ref = refs[:3]
    text_out_refs = refs[3:-1]
    text_part_ref = refs[-1]
    squares, own, width = keep_ref.shape
    scale = scale_ref[0]
    col = col_ref[...]
    rows = jnp.concatenate([row_ref[...]] * 4, axis=0)
    text = text_ref[...]
    pairs = [(same_ref, other_ref), (keep_ref, send_ref)]
    pairs[1] = tuple(ref.reshape(squares * own, width) for ref in pairs[1])
    text_part = None
    for at, (image_ref, out_ref), part in chunks(pairs):
        image = image_ref[part, :]
        here = slice(at, at + image.shape[0])
        row = jnp.transpose(rows[:, here])
        teach = teach_ref[here, :]
        learn = scale * product(image, text)
        rows_part = jnp.exp(learn - row[:, 1:2]) - jnp.exp(teach - row[:, 0:1])
        cols_part = jnp.exp(learn - col[1:2, :]) - jnp.exp(teach - col[0:1, :])
        weight = (0.5 * (rows_part + cols_part)).astype(BF16)
        image_part = scale * jnp.dot(weight, text, preferred_element_type=F32)
        out_ref[part, :] = image_part.astype(out_ref.dtype)
        piece = scale * lax.dot_general(
            weight, image, (((0,), (0,)), ((), ())), preferred_element_type=F32
        )
        text_part = piece if text_part is None else text_part + piece
    text_part_ref[...] = text_part
    z = z_ref[0]
    own_text_ref[...] = text_part_ref[pl.ds(pl.multiple_of(z * own, own), own), :]
    for s, ref in enumerate(text_out_refs):
        row = pl.multiple_of(jnp.bitwise_xor(z, s + 1) * own, own)
        ref[...] = text_part_ref[pl.ds(row, own), :].astype(BF16)


def back_norm(grad, raw):
    unit, inverse = unit_rows(raw)
    return inverse * (grad - unit * jnp.sum(unit * grad, axis=-1, keepdims=True))


def pair_kernel(square_ref, kept_ref, received_ref, *refs):
    for s, ref in enumerate(refs):
        at = jnp.bitwise_xor(square_ref[0], s)
        ref[...] = (kept_ref[at] + received_ref[at].astype(F32)).astype(ref.dtype)


def total_of(refs):
    total = refs[0][...]
    for ref in refs[1:]:
        total = total + ref[...].astype(F32)
    return total


def sum_kernel(*refs):
    refs[-1][...] = total_of(refs[:-1])


def back_kernel(raw_image_ref, raw_text_ref, text_ref, *refs):
    image_out_ref, text_out_ref = refs[-2:]
    text_out_ref[...] = back_norm(text_ref[...], raw_text_ref[...])
    image_out_ref[...] = back_norm(total_of(refs[:-2]), raw_image_ref[...])


def shaped(shape, dtype):
    return jax.ShapeDtypeStruct(shape, dtype)


def call(kernel, outs, ins, specs, out_spec, scratch=(), grant=16, flops=1 << 20):
    return pl.pallas_call(
        kernel,
        out_shape=outs,
        in_specs=specs,
        out_specs=jax.tree.map(lambda _: out_spec, outs),
        scratch_shapes=list(scratch),
        compiler_params=pltpu.CompilerParams(vmem_limit_bytes=grant << 20),
        cost_estimate=pl.CostEstimate(flops=flops, bytes_accessed=1 << 20, transcendentals=0),
    )(*ins)


def bits(count):
    return [1 << i for i in reversed(range((count - 1).bit_length()))]


def make_body(squares, depth):
    plane = 2 * squares
    vmem = pl.BlockSpec(memory_space=pltpu.VMEM)
    smem = pl.BlockSpec(memory_space=pltpu.SMEM)

    def to_line(value, step):
        return lax.ppermute(value, LINE, [(z, z ^ step) for z in range(depth)])

    def to_square(value, step):
        return lax.ppermute(value, SQUARE, [(q, q ^ step) for q in range(squares)])

    def gather_square(value):
        first = bits(squares)
        blocks = dict(zip([0] + first, [value] + [to_square(value, s) for s in first]))
        for s in sorted(set(range(squares)) - set(blocks), key=lambda s: bin(s).count("1")):
            hop = s & -s
            blocks[s] = to_square(blocks[s ^ hop], hop)
        return [blocks[s] for s in range(squares)]

    def gather_line(student, teacher):
        far = bits(depth)[:-1]
        parts = [student, teacher]
        units = {s: [to_line(part, s) for part in parts] for s in far}
        near = to_line(side_by_side(student, teacher), 1)
        for s in far:
            units[s][0], near = lax.optimization_barrier((units[s][0], near))
            for k, raw in enumerate(units[s]):
                units[s][k] = call(
                    unit_kernel, shaped(raw.shape, BF16), (raw,), [vmem], vmem, flops=(FEW, SOME)[k]
                )
        rest = set(range(2, depth)) - set(far)
        for s in sorted(rest, key=lambda s: bin(s).count("1")):
            hop = s & -s
            units[s] = [to_line(part, hop) for part in units[s ^ hop]]
        return near, units

    def to_sibling(value):
        return lax.ppermute(value, "core", [(0, 1), (1, 0)])

    def body(student_image, student_text, teacher_image, teacher_text, teacher_scale, student_scale):
        own, width = student_image.shape
        both = width + teacher_image.shape[1]
        images, texts = plane * own, depth * own
        square = lax.axis_index("y") * lax.axis_size("x") + lax.axis_index("x")
        square = square.astype(jnp.int32).reshape(1)
        z = lax.axis_index("z").astype(jnp.int32).reshape(1)
        teacher_scale = teacher_scale.reshape(1)
        student_scale = student_scale.reshape(1)
        grant = 16 if images * texts <= 512 * 256 else 56

        raw_image = side_by_side(student_image, teacher_image)
        blocks = gather_square(raw_image)
        near, units = gather_line(student_text, teacher_text)
        raw_texts = [student_text, teacher_text, near] + sum(units.values(), [])

        pupil_text, master_text = call(
            functools.partial(text_unit_kernel, tuple(units)),
            (shaped((texts, width), BF16), shaped((texts, both - width), BF16)),
            (z, *raw_texts),
            [smem] + [vmem] * len(raw_texts),
            vmem,
            grant=grant,
            flops=MANY,
        )
        half = squares * own
        pupil, master = call(
            image_unit_kernel,
            (shaped((half, width), BF16), shaped((half, both - width), BF16)),
            (square, *blocks),
            [smem] + [vmem] * squares,
            vmem,
            grant=grant,
            flops=MANY,
        )
        pupils, masters = (pupil, to_sibling(pupil)), (master, to_sibling(master))
        teach, row_lse, col_lse = call(
            logits_kernel,
            (shaped((images, texts), F32), shaped((2, images), F32), shaped((2, texts), F32)),
            (teacher_scale, student_scale, pupil_text, master_text, *pupils, *masters),
            [smem, smem] + [vmem] * 6,
            vmem,
            grant=grant,
        )

        def joined(parts, flops):
            out = shaped(parts[0].shape, F32)
            return call(join_kernel, out, parts, [vmem] * len(parts), vmem, flops=flops)

        row_lse = call(
            join_sibling_kernel,
            shaped(row_lse.shape, F32),
            (row_lse, to_sibling(row_lse)),
            [vmem] * 2,
            vmem,
        )
        row_lses = [to_square(row_lse, s) for s in range(1, squares)]
        row_lse = joined([row_lse, *row_lses], MANY)
        for s in bits(depth):
            col_lse = joined([col_lse, to_line(col_lse, s)], FEW if s == 1 else SOME)
        block = shaped((own, width), F32)
        sent = shaped((own, width), BF16)
        kept, for_sibling, own_text, *for_line = call(
            weight_kernel,
            (shaped((squares, own, width), F32), shaped((squares, own, width), BF16), block)
            + (sent,) * (depth - 1),
            (z, student_scale, teach, *pupils, pupil_text, col_lse, row_lse),
            [smem] * 2 + [vmem] * 6,
            vmem,
            (pltpu.VMEM((texts, width), F32),),
            grant,
        )
        text_parts = [to_line(part, s + 1) for s, part in enumerate(for_line)]
        text_grad = call(sum_kernel, block, (own_text, *text_parts), [vmem] * depth, vmem, flops=MANY)
        own_image, *for_square = call(
            pair_kernel,
            (block,) + (sent,) * (squares - 1),
            (square, kept, to_sibling(for_sibling)),
            [smem] + [vmem] * 2,
            vmem,
        )
        image_parts = [to_square(part, s + 1) for s, part in reversed(list(enumerate(for_square)))]
        return call(
            back_kernel,
            (block, block),
            (student_image, student_text, text_grad, own_image, *image_parts),
            [vmem] * (3 + squares),
            vmem,
        )

    return body


def solution(mesh):
    named = physical_mesh(mesh)
    split = P(EVERY, None)
    return jax.shard_map(
        make_body(named.shape["y"] * named.shape["x"], named.shape["z"]),
        mesh=named,
        in_specs=(split, split, split, split, P(), P()),
        out_specs=(split, split),
        check_vma=False,
    )
```

```python
import functools

import jax
import jax.numpy as jnp
from jax import lax
from jax.experimental import pallas as pl
from jax.experimental.pallas import tpu as pltpu
from jax.sharding import Mesh, PartitionSpec as P

EPSILON = 1e-12
SQUARE = ("y", "x")
LINE = "z"
EVERY = ("y", "core", "z", "x")
F32 = jnp.float32
BF16 = jnp.bfloat16
FEW, SOME, MANY = 1 << 10, 1 << 31, 1 << 35


def physical_mesh(mesh):
    rows, cols = mesh.shape["row"], mesh.shape["col"]
    side = rows // 2
    wide = side if cols % side == 0 else 1
    return Mesh(mesh.devices.reshape(side, 2, cols // wide, wide), EVERY)


def unit_rows(raw):
    values = raw.astype(F32)
    inverse = lax.rsqrt(jnp.sum(values * values, axis=-1, keepdims=True) + EPSILON)
    return (values * inverse, inverse)


def side_by_side(left, right):
    lowest = jnp.array(-jnp.inf, left.dtype)
    left_width, right_width = left.shape[1], right.shape[1]
    return jnp.maximum(
        lax.pad(left, lowest, ((0, 0, 0), (0, right_width, 0))),
        lax.pad(right, lowest, ((0, 0, 0), (left_width, 0, 0))),
    )


def put_units(block, pupil_ref, master_ref, at):
    at = pl.multiple_of(at, block.shape[0])
    own, width = block.shape[0], pupil_ref.shape[1]
    pupil_ref[pl.ds(at, own), :] = unit_rows(block[:, :width])[0].astype(BF16)
    master_ref[pl.ds(at, own), :] = unit_rows(block[:, width:])[0].astype(BF16)


def image_unit_kernel(square_ref, *refs):
    pupil_ref, master_ref = refs[-2:]
    own = refs[0].shape[0]
    for s, ref in enumerate(refs[:-2]):
        row = pl.multiple_of(jnp.bitwise_xor(square_ref[0], s) * own, own)
        put_units(ref[...], pupil_ref, master_ref, row)


def unit_kernel(raw_ref, out_ref):
    out_ref[...] = unit_rows(raw_ref[...])[0].astype(BF16)


def text_unit_kernel(distances, z_ref, student_ref, teacher_ref, near_ref, *refs):
    pupil_ref, master_ref = refs[-2:]
    own = near_ref.shape[0]

    def place(s):
        return pl.ds(pl.multiple_of(jnp.bitwise_xor(z_ref[0], s) * own, own), own)

    put_units(near_ref[...], pupil_ref, master_ref, jnp.bitwise_xor(z_ref[0], 1) * own)
    unit_kernel(student_ref, pupil_ref.at[place(0)])
    unit_kernel(teacher_ref, master_ref.at[place(0)])
    for k, s in enumerate(distances):
        pupil_ref[place(s), :] = refs[2 * k][...]
        master_ref[place(s), :] = refs[2 * k + 1][...]


def product(left, right):
    return lax.dot_general(left, right, (((1,), (1,)), ((), ())), preferred_element_type=F32)


def block_lse(logits):
    peak = jnp.max(logits, axis=0, keepdims=True)
    return peak + jnp.log(jnp.sum(jnp.exp(logits - peak), axis=0, keepdims=True))


def join_lse(parts):
    top = functools.reduce(jnp.maximum, parts)
    return top + jnp.log(sum(jnp.exp(p - top) for p in parts))


def chunks(pairs):
    half = pairs[0][0].shape[0]
    step = min(512, half)
    return [
        (k * half + at, [pair[k] for pair in pairs], slice(at, at + step))
        for k in range(2)
        for at in range(0, half, step)
    ]


def logits_kernel(
    teacher_scale_ref, student_scale_ref, pupil_text_ref, master_text_ref, pupil_same_ref,
    pupil_other_ref, master_same_ref, master_other_ref, teach_ref, rows_ref, cols_ref,
):
    for k, (scale_ref, pair, text_ref) in enumerate(
        (
            (teacher_scale_ref, (master_same_ref, master_other_ref), master_text_ref),
            (student_scale_ref, (pupil_same_ref, pupil_other_ref), pupil_text_ref),
        )
    ):
        scale = scale_ref[0]
        text = text_ref[...]
        columns = []
        for at, (ref,), part in chunks([pair]):
            image = ref[part, :]
            rows = slice(at, at + image.shape[0])
            logits = scale * product(image, text)
            if k == 0:
                teach_ref[rows, :] = logits
            columns.append(block_lse(logits))
            rows_ref[k : k + 1, rows] = block_lse(scale * product(text, image))
        cols_ref[k : k + 1, :] = join_lse(columns)


def join_kernel(*refs):
    refs[-1][...] = join_lse([ref[...] for ref in refs[:-1]])


def join_sibling_kernel(own_ref, other_ref, out_ref):
    half = own_ref.shape[1] // 2
    for here, there in ((slice(0, half), slice(half, None)), (slice(half, None), slice(0, half))):
        out_ref[:, here] = join_lse([own_ref[:, here], other_ref[:, there]])


def weight_kernel(z_ref, scale_ref, teach_ref, same_ref, other_ref, text_ref, col_ref, row_ref, *refs):
    keep_ref, send_ref, own_text_ref = refs[:3]
    text_out_refs = refs[3:-1]
    text_part_ref = refs[-1]
    squares, own, width = keep_ref.shape
    scale = scale_ref[0]
    col = col_ref[...]
    rows = jnp.concatenate([row_ref[...]] * 4, axis=0)
    text = text_ref[...]
    pairs = [(same_ref, other_ref), (keep_ref, send_ref)]
    pairs[1] = tuple(ref.reshape(squares * own, width) for ref in pairs[1])
    text_part = None
    for at, (image_ref, out_ref), part in chunks(pairs):
        image = image_ref[part, :]
        here = slice(at, at + image.shape[0])
        row = jnp.transpose(rows[:, here])
        teach = teach_ref[here, :]
        learn = scale * product(image, text)
        rows_part = jnp.exp(learn - row[:, 1:2]) - jnp.exp(teach - row[:, 0:1])
        cols_part = jnp.exp(learn - col[1:2, :]) - jnp.exp(teach - col[0:1, :])
        weight = (0.5 * (rows_part + cols_part)).astype(BF16)
        image_part = scale * jnp.dot(weight, text, preferred_element_type=F32)
        out_ref[part, :] = image_part.astype(out_ref.dtype)
        piece = scale * lax.dot_general(
            weight, image, (((0,), (0,)), ((), ())), preferred_element_type=F32
        )
        text_part = piece if text_part is None else text_part + piece
    text_part_ref[...] = text_part
    z = z_ref[0]
    own_text_ref[...] = text_part_ref[pl.ds(pl.multiple_of(z * own, own), own), :]
    for s, ref in enumerate(text_out_refs):
        row = pl.multiple_of(jnp.bitwise_xor(z, s + 1) * own, own)
        ref[...] = text_part_ref[pl.ds(row, own), :].astype(BF16)


def back_norm(grad, raw):
    unit, inverse = unit_rows(raw)
    return inverse * (grad - unit * jnp.sum(unit * grad, axis=-1, keepdims=True))


def pair_kernel(square_ref, kept_ref, received_ref, *refs):
    for s, ref in enumerate(refs):
        at = jnp.bitwise_xor(square_ref[0], s)
        ref[...] = (kept_ref[at] + received_ref[at].astype(F32)).astype(ref.dtype)


def total_of(refs):
    total = refs[0][...]
    for ref in refs[1:]:
        total = total + ref[...].astype(F32)
    return total


def sum_kernel(*refs):
    refs[-1][...] = total_of(refs[:-1])


def back_kernel(raw_image_ref, raw_text_ref, text_ref, *refs):
    image_out_ref, text_out_ref = refs[-2:]
    text_out_ref[...] = back_norm(text_ref[...], raw_text_ref[...])
    image_out_ref[...] = back_norm(total_of(refs[:-2]), raw_image_ref[...])


def shaped(shape, dtype):
    return jax.ShapeDtypeStruct(shape, dtype)


def call(kernel, outs, ins, specs, out_spec, scratch=(), grant=16, flops=1 << 20):
    return pl.pallas_call(
        kernel,
        out_shape=outs,
        in_specs=specs,
        out_specs=jax.tree.map(lambda _: out_spec, outs),
        scratch_shapes=list(scratch),
        compiler_params=pltpu.CompilerParams(vmem_limit_bytes=grant << 20),
        cost_estimate=pl.CostEstimate(flops=flops, bytes_accessed=1 << 20, transcendentals=0),
    )(*ins)


def bits(count):
    return [1 << i for i in reversed(range((count - 1).bit_length()))]


def make_body(squares, depth):
    plane = 2 * squares
    vmem = pl.BlockSpec(memory_space=pltpu.VMEM)
    smem = pl.BlockSpec(memory_space=pltpu.SMEM)

    def to_line(value, step):
        return lax.ppermute(value, LINE, [(z, z ^ step) for z in range(depth)])

    def to_square(value, step):
        return lax.ppermute(value, SQUARE, [(q, q ^ step) for q in range(squares)])

    def gather_square(value):
        first = bits(squares)
        blocks = dict(zip([0] + first, [value] + [to_square(value, s) for s in first]))
        for s in sorted(set(range(squares)) - set(blocks), key=lambda s: bin(s).count("1")):
            hop = s & -s
            blocks[s] = to_square(blocks[s ^ hop], hop)
        return [blocks[s] for s in range(squares)]

    def gather_line(student, teacher):
        far = bits(depth)[:-1]
        parts = [student, teacher]
        units = {s: [to_line(part, s) for part in parts] for s in far}
        near = to_line(side_by_side(student, teacher), 1)
        for s in far:
            units[s][0], near = lax.optimization_barrier((units[s][0], near))
            for k, raw in enumerate(units[s]):
                units[s][k] = call(
                    unit_kernel, shaped(raw.shape, BF16), (raw,), [vmem], vmem, flops=(FEW, SOME)[k]
                )
        rest = set(range(2, depth)) - set(far)
        for s in sorted(rest, key=lambda s: bin(s).count("1")):
            hop = s & -s
            units[s] = [to_line(part, hop) for part in units[s ^ hop]]
        return near, units

    def to_sibling(value):
        return lax.ppermute(value, "core", [(0, 1), (1, 0)])

    def body(student_image, student_text, teacher_image, teacher_text, teacher_scale, student_scale):
        own, width = student_image.shape
        both = width + teacher_image.shape[1]
        images, texts = plane * own, depth * own
        square = lax.axis_index("y") * lax.axis_size("x") + lax.axis_index("x")
        square = square.astype(jnp.int32).reshape(1)
        z = lax.axis_index("z").astype(jnp.int32).reshape(1)
        teacher_scale = teacher_scale.reshape(1)
        student_scale = student_scale.reshape(1)
        grant = 16 if images * texts <= 512 * 256 else 56

        raw_image = side_by_side(student_image, teacher_image)
        blocks = gather_square(raw_image)
        near, units = gather_line(student_text, teacher_text)
        raw_texts = [student_text, teacher_text, near] + sum(units.values(), [])

        pupil_text, master_text = call(
            functools.partial(text_unit_kernel, tuple(units)),
            (shaped((texts, width), BF16), shaped((texts, both - width), BF16)),
            (z, *raw_texts),
            [smem] + [vmem] * len(raw_texts),
            vmem,
            grant=grant,
            flops=MANY,
        )
        half = squares * own
        pupil, master = call(
            image_unit_kernel,
            (shaped((half, width), BF16), shaped((half, both - width), BF16)),
            (square, *blocks),
            [smem] + [vmem] * squares,
            vmem,
            grant=grant,
            flops=MANY,
        )
        pupils, masters = (pupil, to_sibling(pupil)), (master, to_sibling(master))
        teach, row_lse, col_lse = call(
            logits_kernel,
            (shaped((images, texts), F32), shaped((2, images), F32), shaped((2, texts), F32)),
            (teacher_scale, student_scale, pupil_text, master_text, *pupils, *masters),
            [smem, smem] + [vmem] * 6,
            vmem,
            grant=grant,
        )

        def joined(parts, flops):
            out = shaped(parts[0].shape, F32)
            return call(join_kernel, out, parts, [vmem] * len(parts), vmem, flops=flops)

        row_lse = call(
            join_sibling_kernel,
            shaped(row_lse.shape, F32),
            (row_lse, to_sibling(row_lse)),
            [vmem] * 2,
            vmem,
        )
        row_lses = {s: to_square(row_lse, s) for s in range(1, squares)}
        near = [row_lses.pop(s) for s in bits(squares)[::-1]]
        row_lse = joined([row_lse, *row_lses.values()], SOME)
        row_lse = joined([row_lse, *near], MANY)
        for s in bits(depth):
            col_lse = joined([col_lse, to_line(col_lse, s)], FEW if s == 1 else SOME)
        block = shaped((own, width), F32)
        sent = shaped((own, width), BF16)
        kept, for_sibling, own_text, *for_line = call(
            weight_kernel,
            (shaped((squares, own, width), F32), shaped((squares, own, width), BF16), block)
            + (sent,) * (depth - 1),
            (z, student_scale, teach, *pupils, pupil_text, col_lse, row_lse),
            [smem] * 2 + [vmem] * 6,
            vmem,
            (pltpu.VMEM((texts, width), F32),),
            grant,
        )
        text_parts = [to_line(part, s + 1) for s, part in enumerate(for_line)]
        text_grad = call(sum_kernel, block, (own_text, *text_parts), [vmem] * depth, vmem, flops=MANY)
        own_image, *for_square = call(
            pair_kernel,
            (block,) + (sent,) * (squares - 1),
            (square, kept, to_sibling(for_sibling)),
            [smem] + [vmem] * 2,
            vmem,
        )
        image_parts = [to_square(part, s + 1) for s, part in reversed(list(enumerate(for_square)))]
        return call(
            back_kernel,
            (block, block),
            (student_image, student_text, text_grad, own_image, *image_parts),
            [vmem] * (3 + squares),
            vmem,
        )

    return body


def solution(mesh):
    named = physical_mesh(mesh)
    split = P(EVERY, None)
    return jax.shard_map(
        make_body(named.shape["y"] * named.shape["x"], named.shape["z"]),
        mesh=named,
        in_specs=(split, split, split, split, P(), P()),
        out_specs=(split, split),
        check_vma=False,
    )
```

```python
import functools

import jax
import jax.numpy as jnp
from jax import lax
from jax.experimental import pallas as pl
from jax.experimental.pallas import tpu as pltpu
from jax.sharding import Mesh, PartitionSpec as P

EPSILON = 1e-12
SQUARE = ("y", "x")
LINE = "z"
EVERY = ("y", "core", "z", "x")
F32 = jnp.float32
BF16 = jnp.bfloat16
FEW, SOME, MANY = 1 << 10, 1 << 31, 1 << 35


def physical_mesh(mesh):
    rows, cols = mesh.shape["row"], mesh.shape["col"]
    side = rows // 2
    wide = side if cols % side == 0 else 1
    return Mesh(mesh.devices.reshape(side, 2, cols // wide, wide), EVERY)


def unit_rows(raw):
    values = raw.astype(F32)
    inverse = lax.rsqrt(jnp.sum(values * values, axis=-1, keepdims=True) + EPSILON)
    return (values * inverse, inverse)


def side_by_side(left, right):
    lowest = jnp.array(-jnp.inf, left.dtype)
    left_width, right_width = left.shape[1], right.shape[1]
    return jnp.maximum(
        lax.pad(left, lowest, ((0, 0, 0), (0, right_width, 0))),
        lax.pad(right, lowest, ((0, 0, 0), (left_width, 0, 0))),
    )


def put_units(block, pupil_ref, master_ref, at):
    at = pl.multiple_of(at, block.shape[0])
    own, width = block.shape[0], pupil_ref.shape[1]
    pupil_ref[pl.ds(at, own), :] = unit_rows(block[:, :width])[0].astype(BF16)
    master_ref[pl.ds(at, own), :] = unit_rows(block[:, width:])[0].astype(BF16)


def image_unit_kernel(square_ref, *refs):
    pupil_ref, master_ref = refs[-2:]
    own = refs[0].shape[0]
    for s, ref in enumerate(refs[:-2]):
        row = pl.multiple_of(jnp.bitwise_xor(square_ref[0], s) * own, own)
        put_units(ref[...], pupil_ref, master_ref, row)


def unit_kernel(raw_ref, out_ref):
    out_ref[...] = unit_rows(raw_ref[...])[0].astype(BF16)


def text_unit_kernel(distances, z_ref, student_ref, teacher_ref, near_ref, *refs):
    pupil_ref, master_ref = refs[-2:]
    own = near_ref.shape[0]

    def place(s):
        return pl.ds(pl.multiple_of(jnp.bitwise_xor(z_ref[0], s) * own, own), own)

    put_units(near_ref[...], pupil_ref, master_ref, jnp.bitwise_xor(z_ref[0], 1) * own)
    unit_kernel(student_ref, pupil_ref.at[place(0)])
    unit_kernel(teacher_ref, master_ref.at[place(0)])
    for k, s in enumerate(distances):
        pupil_ref[place(s), :] = refs[2 * k][...]
        master_ref[place(s), :] = refs[2 * k + 1][...]


def product(left, right):
    return lax.dot_general(left, right, (((1,), (1,)), ((), ())), preferred_element_type=F32)


def block_lse(logits):
    peak = jnp.max(logits, axis=0, keepdims=True)
    return peak + jnp.log(jnp.sum(jnp.exp(logits - peak), axis=0, keepdims=True))


def join_lse(parts):
    top = functools.reduce(jnp.maximum, parts)
    return top + jnp.log(sum(jnp.exp(p - top) for p in parts))


def chunks(pairs):
    half = pairs[0][0].shape[0]
    step = min(512, half)
    return [
        (k * half + at, [pair[k] for pair in pairs], slice(at, at + step))
        for k in range(2)
        for at in range(0, half, step)
    ]


def logits_kernel(
    teacher_scale_ref, student_scale_ref, pupil_text_ref, master_text_ref, pupil_same_ref,
    pupil_other_ref, master_same_ref, master_other_ref, teach_ref, rows_ref, cols_ref,
):
    for k, (scale_ref, pair, text_ref) in enumerate(
        (
            (teacher_scale_ref, (master_same_ref, master_other_ref), master_text_ref),
            (student_scale_ref, (pupil_same_ref, pupil_other_ref), pupil_text_ref),
        )
    ):
        scale = scale_ref[0]
        text = text_ref[...]
        columns = []
        for at, (ref,), part in chunks([pair]):
            image = ref[part, :]
            rows = slice(at, at + image.shape[0])
            logits = scale * product(image, text)
            if k == 0:
                teach_ref[rows, :] = logits
            columns.append(block_lse(logits))
            rows_ref[k : k + 1, rows] = block_lse(scale * product(text, image))
        cols_ref[k : k + 1, :] = join_lse(columns)


def join_kernel(*refs):
    refs[-1][...] = join_lse([ref[...] for ref in refs[:-1]])


def join_sibling_kernel(own_ref, other_ref, out_ref):
    half = own_ref.shape[1] // 2
    for here, there in ((slice(0, half), slice(half, None)), (slice(half, None), slice(0, half))):
        out_ref[:, here] = join_lse([own_ref[:, here], other_ref[:, there]])


def weight_kernel(z_ref, scale_ref, teach_ref, same_ref, other_ref, text_ref, col_ref, row_ref, *refs):
    keep_ref, send_ref, own_text_ref = refs[:3]
    text_out_refs = refs[3:-1]
    text_part_ref = refs[-1]
    squares, own, width = keep_ref.shape
    scale = scale_ref[0]
    col = col_ref[...]
    rows = jnp.concatenate([row_ref[...]] * 4, axis=0)
    text = text_ref[...]
    half = squares * own
    pupils = jnp.concatenate([same_ref[...], other_ref[...]], axis=0)
    step = min(512, 2 * half)
    parts = [ref.reshape(half, width) for ref in (keep_ref, send_ref)]
    text_part = None
    for at in range(0, 2 * half, step):
        image = pupils[at : at + step]
        row = jnp.transpose(rows[:, at : at + step])
        teach = teach_ref[at : at + step, :]
        learn = scale * product(image, text)
        rows_part = jnp.exp(learn - row[:, 1:2]) - jnp.exp(teach - row[:, 0:1])
        cols_part = jnp.exp(learn - col[1:2, :]) - jnp.exp(teach - col[0:1, :])
        weight = (0.5 * (rows_part + cols_part)).astype(BF16)
        image_part = scale * jnp.dot(weight, text, preferred_element_type=F32)
        for here in range(at, at + step, min(half, step)):
            ref = parts[here // half]
            first = here % half
            piece = image_part[here - at : here - at + min(half, step)]
            ref[first : first + piece.shape[0], :] = piece.astype(ref.dtype)
        piece = scale * lax.dot_general(
            weight, image, (((0,), (0,)), ((), ())), preferred_element_type=F32
        )
        text_part = piece if text_part is None else text_part + piece
    text_part_ref[...] = text_part
    z = z_ref[0]
    own_text_ref[...] = text_part_ref[pl.ds(pl.multiple_of(z * own, own), own), :]
    for s, ref in enumerate(text_out_refs):
        row = pl.multiple_of(jnp.bitwise_xor(z, s + 1) * own, own)
        ref[...] = text_part_ref[pl.ds(row, own), :].astype(BF16)


def back_norm(grad, raw):
    unit, inverse = unit_rows(raw)
    return inverse * (grad - unit * jnp.sum(unit * grad, axis=-1, keepdims=True))


def pair_kernel(square_ref, kept_ref, received_ref, *refs):
    for s, ref in enumerate(refs):
        at = jnp.bitwise_xor(square_ref[0], s)
        ref[...] = (kept_ref[at] + received_ref[at].astype(F32)).astype(ref.dtype)


def total_of(refs):
    total = refs[0][...]
    for ref in refs[1:]:
        total = total + ref[...].astype(F32)
    return total


def sum_kernel(*refs):
    refs[-1][...] = total_of(refs[:-1])


def back_kernel(raw_image_ref, raw_text_ref, text_ref, *refs):
    image_out_ref, text_out_ref = refs[-2:]
    text_out_ref[...] = back_norm(text_ref[...], raw_text_ref[...])
    image_out_ref[...] = back_norm(total_of(refs[:-2]), raw_image_ref[...])


def shaped(shape, dtype):
    return jax.ShapeDtypeStruct(shape, dtype)


def call(kernel, outs, ins, specs, out_spec, scratch=(), grant=16, flops=1 << 20):
    return pl.pallas_call(
        kernel,
        out_shape=outs,
        in_specs=specs,
        out_specs=jax.tree.map(lambda _: out_spec, outs),
        scratch_shapes=list(scratch),
        compiler_params=pltpu.CompilerParams(vmem_limit_bytes=grant << 20),
        cost_estimate=pl.CostEstimate(flops=flops, bytes_accessed=1 << 20, transcendentals=0),
    )(*ins)


def bits(count):
    return [1 << i for i in reversed(range((count - 1).bit_length()))]


def make_body(squares, depth):
    plane = 2 * squares
    vmem = pl.BlockSpec(memory_space=pltpu.VMEM)
    smem = pl.BlockSpec(memory_space=pltpu.SMEM)

    def to_line(value, step):
        return lax.ppermute(value, LINE, [(z, z ^ step) for z in range(depth)])

    def to_square(value, step):
        return lax.ppermute(value, SQUARE, [(q, q ^ step) for q in range(squares)])

    def gather_square(value):
        first = bits(squares)
        blocks = dict(zip([0] + first, [value] + [to_square(value, s) for s in first]))
        for s in sorted(set(range(squares)) - set(blocks), key=lambda s: bin(s).count("1")):
            hop = s & -s
            blocks[s] = to_square(blocks[s ^ hop], hop)
        return [blocks[s] for s in range(squares)]

    def gather_line(student, teacher):
        far = bits(depth)[:-1]
        parts = [student, teacher]
        units = {s: [to_line(part, s) for part in parts] for s in far}
        near = to_line(side_by_side(student, teacher), 1)
        for s in far:
            units[s][0], near = lax.optimization_barrier((units[s][0], near))
            for k, raw in enumerate(units[s]):
                units[s][k] = call(
                    unit_kernel, shaped(raw.shape, BF16), (raw,), [vmem], vmem, flops=(FEW, SOME)[k]
                )
        rest = set(range(2, depth)) - set(far)
        for s in sorted(rest, key=lambda s: bin(s).count("1")):
            hop = s & -s
            units[s] = [to_line(part, hop) for part in units[s ^ hop]]
        return near, units

    def to_sibling(value):
        return lax.ppermute(value, "core", [(0, 1), (1, 0)])

    def body(student_image, student_text, teacher_image, teacher_text, teacher_scale, student_scale):
        own, width = student_image.shape
        both = width + teacher_image.shape[1]
        images, texts = plane * own, depth * own
        square = lax.axis_index("y") * lax.axis_size("x") + lax.axis_index("x")
        square = square.astype(jnp.int32).reshape(1)
        z = lax.axis_index("z").astype(jnp.int32).reshape(1)
        teacher_scale = teacher_scale.reshape(1)
        student_scale = student_scale.reshape(1)
        grant = 16 if images * texts <= 512 * 256 else 56

        raw_image = side_by_side(student_image, teacher_image)
        blocks = gather_square(raw_image)
        near, units = gather_line(student_text, teacher_text)
        raw_texts = [student_text, teacher_text, near] + sum(units.values(), [])

        pupil_text, master_text = call(
            functools.partial(text_unit_kernel, tuple(units)),
            (shaped((texts, width), BF16), shaped((texts, both - width), BF16)),
            (z, *raw_texts),
            [smem] + [vmem] * len(raw_texts),
            vmem,
            grant=grant,
            flops=MANY,
        )
        half = squares * own
        pupil, master = call(
            image_unit_kernel,
            (shaped((half, width), BF16), shaped((half, both - width), BF16)),
            (square, *blocks),
            [smem] + [vmem] * squares,
            vmem,
            grant=grant,
            flops=MANY,
        )
        pupils, masters = (pupil, to_sibling(pupil)), (master, to_sibling(master))
        teach, row_lse, col_lse = call(
            logits_kernel,
            (shaped((images, texts), F32), shaped((2, images), F32), shaped((2, texts), F32)),
            (teacher_scale, student_scale, pupil_text, master_text, *pupils, *masters),
            [smem, smem] + [vmem] * 6,
            vmem,
            grant=grant,
        )

        def joined(parts, flops):
            out = shaped(parts[0].shape, F32)
            return call(join_kernel, out, parts, [vmem] * len(parts), vmem, flops=flops)

        row_lse = call(
            join_sibling_kernel,
            shaped(row_lse.shape, F32),
            (row_lse, to_sibling(row_lse)),
            [vmem] * 2,
            vmem,
        )
        row_lses = [to_square(row_lse, s) for s in range(1, squares)]
        row_lse = joined([row_lse, *row_lses], MANY)
        for s in bits(depth):
            col_lse = joined([col_lse, to_line(col_lse, s)], FEW if s == 1 else SOME)
        block = shaped((own, width), F32)
        sent = shaped((own, width), BF16)
        kept, for_sibling, own_text, *for_line = call(
            weight_kernel,
            (shaped((squares, own, width), F32), shaped((squares, own, width), BF16), block)
            + (sent,) * (depth - 1),
            (z, student_scale, teach, *pupils, pupil_text, col_lse, row_lse),
            [smem] * 2 + [vmem] * 6,
            vmem,
            (pltpu.VMEM((texts, width), F32),),
            grant,
        )
        text_parts = [to_line(part, s + 1) for s, part in enumerate(for_line)]
        text_grad = call(sum_kernel, block, (own_text, *text_parts), [vmem] * depth, vmem, flops=MANY)
        own_image, *for_square = call(
            pair_kernel,
            (block,) + (sent,) * (squares - 1),
            (square, kept, to_sibling(for_sibling)),
            [smem] + [vmem] * 2,
            vmem,
        )
        image_parts = [to_square(part, s + 1) for s, part in reversed(list(enumerate(for_square)))]
        return call(
            back_kernel,
            (block, block),
            (student_image, student_text, text_grad, own_image, *image_parts),
            [vmem] * (3 + squares),
            vmem,
        )

    return body


def solution(mesh):
    named = physical_mesh(mesh)
    split = P(EVERY, None)
    return jax.shard_map(
        make_body(named.shape["y"] * named.shape["x"], named.shape["z"]),
        mesh=named,
        in_specs=(split, split, split, split, P(), P()),
        out_specs=(split, split),
        check_vma=False,
    )
```

```python
import functools

import jax
import jax.numpy as jnp
from jax import lax
from jax.experimental import pallas as pl
from jax.experimental.pallas import tpu as pltpu
from jax.sharding import Mesh, PartitionSpec as P

EPSILON = 1e-12
SQUARE = ("y", "x")
LINE = "z"
EVERY = ("y", "core", "z", "x")
F32 = jnp.float32
BF16 = jnp.bfloat16
FEW, SOME, MANY = 1 << 10, 1 << 31, 1 << 35


def physical_mesh(mesh):
    rows, cols = mesh.shape["row"], mesh.shape["col"]
    side = rows // 2
    wide = side if cols % side == 0 else 1
    return Mesh(mesh.devices.reshape(side, 2, cols // wide, wide), EVERY)


def unit_rows(raw):
    values = raw.astype(F32)
    inverse = lax.rsqrt(jnp.sum(values * values, axis=-1, keepdims=True) + EPSILON)
    return (values * inverse, inverse)


def side_by_side(left, right):
    lowest = jnp.array(-jnp.inf, left.dtype)
    left_width, right_width = left.shape[1], right.shape[1]
    return jnp.maximum(
        lax.pad(left, lowest, ((0, 0, 0), (0, right_width, 0))),
        lax.pad(right, lowest, ((0, 0, 0), (left_width, 0, 0))),
    )


def put_units(block, pupil_ref, master_ref, at):
    at = pl.multiple_of(at, block.shape[0])
    own, width = block.shape[0], pupil_ref.shape[1]
    pupil_ref[pl.ds(at, own), :] = unit_rows(block[:, :width])[0].astype(BF16)
    master_ref[pl.ds(at, own), :] = unit_rows(block[:, width:])[0].astype(BF16)


def image_unit_kernel(square_ref, *refs):
    pupil_ref, master_ref = refs[-2:]
    own = refs[0].shape[0]
    for s, ref in enumerate(refs[:-2]):
        row = pl.multiple_of(jnp.bitwise_xor(square_ref[0], s) * own, own)
        put_units(ref[...], pupil_ref, master_ref, row)


def unit_kernel(raw_ref, out_ref):
    out_ref[...] = unit_rows(raw_ref[...])[0].astype(BF16)


def text_unit_kernel(distances, z_ref, student_ref, teacher_ref, near_ref, *refs):
    pupil_ref, master_ref = refs[-2:]
    own = near_ref.shape[0]

    def place(s):
        return pl.ds(pl.multiple_of(jnp.bitwise_xor(z_ref[0], s) * own, own), own)

    put_units(near_ref[...], pupil_ref, master_ref, jnp.bitwise_xor(z_ref[0], 1) * own)
    unit_kernel(student_ref, pupil_ref.at[place(0)])
    unit_kernel(teacher_ref, master_ref.at[place(0)])
    for k, s in enumerate(distances):
        pupil_ref[place(s), :] = refs[2 * k][...]
        master_ref[place(s), :] = refs[2 * k + 1][...]


def product(left, right):
    return lax.dot_general(left, right, (((1,), (1,)), ((), ())), preferred_element_type=F32)


def block_lse(logits):
    peak = jnp.max(logits, axis=0, keepdims=True)
    return peak + jnp.log(jnp.sum(jnp.exp(logits - peak), axis=0, keepdims=True))


def join_lse(parts):
    top = functools.reduce(jnp.maximum, parts)
    return top + jnp.log(sum(jnp.exp(p - top) for p in parts))


def chunks(pairs):
    half = pairs[0][0].shape[0]
    step = min(512, half)
    return [
        (k * half + at, [pair[k] for pair in pairs], slice(at, at + step))
        for k in range(2)
        for at in range(0, half, step)
    ]


def logits_kernel(
    teacher_scale_ref, student_scale_ref, pupil_text_ref, master_text_ref, pupil_same_ref,
    pupil_other_ref, master_same_ref, master_other_ref, teach_ref, rows_ref, cols_ref,
):
    for k, (scale_ref, pair, text_ref) in enumerate(
        (
            (teacher_scale_ref, (master_same_ref, master_other_ref), master_text_ref),
            (student_scale_ref, (pupil_same_ref, pupil_other_ref), pupil_text_ref),
        )
    ):
        scale = scale_ref[0]
        text = text_ref[...]
        columns = []
        for at, (ref,), part in chunks([pair]):
            image = ref[part, :]
            rows = slice(at, at + image.shape[0])
            logits = scale * product(image, text)
            if k == 0:
                teach_ref[rows, :] = logits
            columns.append(block_lse(logits))
            rows_ref[k : k + 1, rows] = block_lse(scale * product(text, image))
        cols_ref[k : k + 1, :] = join_lse(columns)


def join_kernel(*refs):
    refs[-1][...] = join_lse([ref[...] for ref in refs[:-1]])


def join_sibling_kernel(own_ref, other_ref, out_ref):
    half = own_ref.shape[1] // 2
    for here, there in ((slice(0, half), slice(half, None)), (slice(half, None), slice(0, half))):
        out_ref[:, here] = join_lse([own_ref[:, here], other_ref[:, there]])


def weight_kernel(z_ref, scale_ref, teach_ref, same_ref, other_ref, text_ref, col_ref, row_ref, *refs):
    keep_ref, send_ref, own_text_ref = refs[:3]
    text_out_refs = refs[3:-1]
    text_part_ref = refs[-1]
    squares, own, width = keep_ref.shape
    scale = scale_ref[0]
    col = col_ref[...]
    rows = jnp.concatenate([row_ref[...]] * 4, axis=0)
    text = text_ref[...]
    half = squares * own
    pupils = jnp.concatenate([same_ref[...], other_ref[...]], axis=0)
    step = min(512, 2 * half)
    parts = [ref.reshape(half, width) for ref in (keep_ref, send_ref)]
    text_part = None
    for at in range(0, 2 * half, step):
        image = pupils[at : at + step]
        row = jnp.transpose(rows[:, at : at + step])
        teach = teach_ref[at : at + step, :]
        learn = scale * product(image, text)
        rows_part = jnp.exp(learn - row[:, 1:2]) - jnp.exp(teach - row[:, 0:1])
        cols_part = jnp.exp(learn - col[1:2, :]) - jnp.exp(teach - col[0:1, :])
        weight = (0.5 * (rows_part + cols_part)).astype(BF16)
        image_part = scale * jnp.dot(weight, text, preferred_element_type=F32)
        for here in range(at, at + step, min(half, step)):
            ref = parts[here // half]
            first = here % half
            piece = image_part[here - at : here - at + min(half, step)]
            ref[first : first + piece.shape[0], :] = piece.astype(ref.dtype)
        piece = scale * lax.dot_general(
            weight, image, (((0,), (0,)), ((), ())), preferred_element_type=F32
        )
        text_part = piece if text_part is None else text_part + piece
    text_part_ref[...] = text_part
    z = z_ref[0]
    own_text_ref[...] = text_part_ref[pl.ds(pl.multiple_of(z * own, own), own), :]
    for s, ref in enumerate(text_out_refs):
        row = pl.multiple_of(jnp.bitwise_xor(z, s + 1) * own, own)
        ref[...] = text_part_ref[pl.ds(row, own), :].astype(BF16)


def back_norm(grad, raw):
    unit, inverse = unit_rows(raw)
    return inverse * (grad - unit * jnp.sum(unit * grad, axis=-1, keepdims=True))


def pair_kernel(square_ref, kept_ref, received_ref, *refs):
    for s, ref in enumerate(refs):
        at = jnp.bitwise_xor(square_ref[0], s)
        ref[...] = (kept_ref[at] + received_ref[at].astype(F32)).astype(ref.dtype)


def total_of(refs):
    total = refs[0][...]
    for ref in refs[1:]:
        total = total + ref[...].astype(F32)
    return total


def sum_kernel(*refs):
    refs[-1][...] = total_of(refs[:-1])


def back_kernel(raw_image_ref, raw_text_ref, text_ref, *refs):
    image_out_ref, text_out_ref = refs[-2:]
    text_out_ref[...] = back_norm(text_ref[...], raw_text_ref[...])
    image_out_ref[...] = back_norm(total_of(refs[:-2]), raw_image_ref[...])


def shaped(shape, dtype):
    return jax.ShapeDtypeStruct(shape, dtype)


def call(kernel, outs, ins, specs, out_spec, scratch=(), grant=16, flops=1 << 20):
    return pl.pallas_call(
        kernel,
        out_shape=outs,
        in_specs=specs,
        out_specs=jax.tree.map(lambda _: out_spec, outs),
        scratch_shapes=list(scratch),
        compiler_params=pltpu.CompilerParams(vmem_limit_bytes=grant << 20),
        cost_estimate=pl.CostEstimate(flops=flops, bytes_accessed=1 << 20, transcendentals=0),
    )(*ins)


def bits(count):
    return [1 << i for i in reversed(range((count - 1).bit_length()))]


def make_body(squares, depth):
    plane = 2 * squares
    vmem = pl.BlockSpec(memory_space=pltpu.VMEM)
    smem = pl.BlockSpec(memory_space=pltpu.SMEM)

    def to_line(value, step):
        return lax.ppermute(value, LINE, [(z, z ^ step) for z in range(depth)])

    def to_square(value, step):
        return lax.ppermute(value, SQUARE, [(q, q ^ step) for q in range(squares)])

    def gather_square(value):
        first = bits(squares)
        blocks = dict(zip([0] + first, [value] + [to_square(value, s) for s in first]))
        for s in sorted(set(range(squares)) - set(blocks), key=lambda s: bin(s).count("1")):
            hop = s & -s
            blocks[s] = to_square(blocks[s ^ hop], hop)
        return [blocks[s] for s in range(squares)]

    def gather_line(student, teacher):
        far = bits(depth)[:-1]
        parts = [student, teacher]
        units = {s: [to_line(part, s) for part in parts] for s in far}
        near = to_line(side_by_side(student, teacher), 1)
        for s in far:
            units[s][0], near = lax.optimization_barrier((units[s][0], near))
            for k, raw in enumerate(units[s]):
                units[s][k] = call(
                    unit_kernel, shaped(raw.shape, BF16), (raw,), [vmem], vmem, flops=(FEW, SOME)[k]
                )
        rest = set(range(2, depth)) - set(far)
        for s in sorted(rest, key=lambda s: bin(s).count("1")):
            hop = s & -s
            units[s] = [to_line(part, hop) for part in units[s ^ hop]]
        return near, units

    def to_sibling(value):
        return lax.ppermute(value, "core", [(0, 1), (1, 0)])

    def body(student_image, student_text, teacher_image, teacher_text, teacher_scale, student_scale):
        own, width = student_image.shape
        both = width + teacher_image.shape[1]
        images, texts = plane * own, depth * own
        square = lax.axis_index("y") * lax.axis_size("x") + lax.axis_index("x")
        square = square.astype(jnp.int32).reshape(1)
        z = lax.axis_index("z").astype(jnp.int32).reshape(1)
        teacher_scale = teacher_scale.reshape(1)
        student_scale = student_scale.reshape(1)
        grant = 16 if images * texts <= 512 * 256 else 56

        raw_image = side_by_side(student_image, teacher_image)
        blocks = gather_square(raw_image)
        near, units = gather_line(student_text, teacher_text)
        raw_texts = [student_text, teacher_text, near] + sum(units.values(), [])

        pupil_text, master_text = call(
            functools.partial(text_unit_kernel, tuple(units)),
            (shaped((texts, width), BF16), shaped((texts, both - width), BF16)),
            (z, *raw_texts),
            [smem] + [vmem] * len(raw_texts),
            vmem,
            grant=grant,
            flops=MANY,
        )
        half = squares * own
        pupil, master = call(
            image_unit_kernel,
            (shaped((half, width), BF16), shaped((half, both - width), BF16)),
            (square, *blocks),
            [smem] + [vmem] * squares,
            vmem,
            grant=grant,
            flops=MANY,
        )
        pupils, masters = (pupil, to_sibling(pupil)), (master, to_sibling(master))
        teach, row_lse, col_lse = call(
            logits_kernel,
            (shaped((images, texts), F32), shaped((2, images), F32), shaped((2, texts), F32)),
            (teacher_scale, student_scale, pupil_text, master_text, *pupils, *masters),
            [smem, smem] + [vmem] * 6,
            vmem,
            grant=grant,
        )

        def joined(parts, flops):
            out = shaped(parts[0].shape, F32)
            return call(join_kernel, out, parts, [vmem] * len(parts), vmem, flops=flops)

        row_lse = call(
            join_sibling_kernel,
            shaped(row_lse.shape, F32),
            (row_lse, to_sibling(row_lse)),
            [vmem] * 2,
            vmem,
        )
        row_lses = [to_square(row_lse, s) for s in range(1, squares)]
        row_lse = joined([row_lse, *row_lses], MANY)
        for s in bits(depth):
            col_lse = joined([col_lse, to_line(col_lse, s)], FEW if s == 1 else SOME)
        block = shaped((own, width), F32)
        sent = shaped((own, width), BF16)
        kept, for_sibling, own_text, *for_line = call(
            weight_kernel,
            (shaped((squares, own, width), F32), shaped((squares, own, width), BF16), block)
            + (sent,) * (depth - 1),
            (z, student_scale, teach, *pupils, pupil_text, col_lse, row_lse),
            [smem] * 2 + [vmem] * 6,
            vmem,
            (pltpu.VMEM((texts, width), F32),),
            grant,
        )
        order = sorted(range(1, depth), key=lambda s: (s != 2, s))
        text_parts = [to_line(for_line[s - 1], s) for s in order]
        text_grad = call(sum_kernel, block, (own_text, *text_parts), [vmem] * depth, vmem, flops=MANY)
        own_image, *for_square = call(
            pair_kernel,
            (block,) + (sent,) * (squares - 1),
            (square, kept, to_sibling(for_sibling)),
            [smem] + [vmem] * 2,
            vmem,
        )
        image_parts = [to_square(part, s + 1) for s, part in reversed(list(enumerate(for_square)))]
        return call(
            back_kernel,
            (block, block),
            (student_image, student_text, text_grad, own_image, *image_parts),
            [vmem] * (3 + squares),
            vmem,
        )

    return body


def solution(mesh):
    named = physical_mesh(mesh)
    split = P(EVERY, None)
    return jax.shard_map(
        make_body(named.shape["y"] * named.shape["x"], named.shape["z"]),
        mesh=named,
        in_specs=(split, split, split, split, P(), P()),
        out_specs=(split, split),
        check_vma=False,
    )
```
